256 devices in a mesh: dp: 8 (over z), label: 32 (over y, x, core).
Axes of the slice: x: 4, y: 4, z: 8, core: 2. Of those that a mesh axis runs over, the one named last changes fastest.
Arguments:
- token_ids: int32 [16384, 32], P(('dp', 'label')), may hold values from 0 to 30463
- token_table: bfloat16 [30464, 768], P('label'), may hold values from -6 to 6
- norm_gain: float32 [768], replicated, may hold values from 0.1 to 1.9
- slab: bfloat16 [65536, 768], P('label'), may hold values from -0.21875 to 0.21875
- shortlist: int32 [16384, 8], P(('dp', 'label')), may hold values from 0 to 511, all different within a row; in each aligned block of 2048 rows (0 to 2047, 2048 to 4095, ...) at most 96 rows name the same one
- positive_offsets: int32 [16384, 2], P(('dp', 'label')), may hold values from 0 to 127
Outputs:
- embed_grad: float32 [16384, 768], P(('dp', 'label'))
- slab_grad: float32 [2048, 32, 768], P('dp', 'label')
The draws below stay inside these ranges and needn't reach their ends.
Inputs may be any that keep to these rules, and one draw needn't show every extreme that they name: `shortlist`: each query names 8 different label blocks. In each aligned block of 2048 queries (one index of dp) no label block is named by more than 96 queries, and some label block by exactly 96. `positive_offsets`: positive p of query q lies in the block shortlist[q, p], at this row of it.
All inputs are finite; a program needn't handle non-finite values.
Results may differ from the reference program's by a relative error of at most 0.003.
Values may be sent and summed in bfloat16 or wider, within the bound.
A program may use at most 64 MiB of HBM per device.

```python
import math
import jax
import jax.numpy as jnp
import numpy as np
from jax import lax

D = 768
VOCAB = 30464
SEQ = 32
K = 8
POS = 2
BLOCK = 128
LAB_DEV = 2048
GCAP = 96
LABEL_SHARDS = 32
GROUP = 2048
QUERIES = 16384
LABELS = 65536
NBLK = 512


def set_ends(drawn, key, least, top_value):
    longest = drawn.shape.index(max(drawn.shape))
    spots = []
    for shift in (0, 1):
        where = [jax.random.randint(jax.random.fold_in(key, axis), (), 0, length) for axis, length in enumerate(drawn.shape)]
        where[longest] = (where[longest] + shift) % drawn.shape[longest]
        spots.append(tuple(where))
    return drawn.at[spots[0]].set(least).at[spots[1]].set(top_value)


def shard_levels(own_key, dims, shards, low, largest):
    gain, own = 1.0, jax.random.fold_in(own_key, 6)
    for dim, shards_of in shards:
        heights = jnp.exp(jax.random.uniform(jax.random.fold_in(own, dim), (shards_of,), jnp.float32, low / len(shards), largest / len(shards)))
        gain = gain * jnp.repeat(heights, dims[dim] // shards_of).reshape([-1 if axis == dim else 1 for axis in range(len(dims))])
    return gain


def rank_bounds(number_of, slope):
    weights = [(1 << 20) // math.isqrt(rank ** slope) + 1 for rank in range(1, number_of + 1)]
    deviation = 1 + sum(weights) // (1 << 30)
    return np.cumsum(np.array([max(1, weight // deviation) for weight in weights]))


def ranked_ids(own_key, dims, count, lean):
    table = rank_bounds(count, lean)
    lot = jax.random.randint(jax.random.fold_in(own_key, 1), dims, 0, int(table[count - 1]))
    grade = jnp.searchsorted(jnp.asarray(table, jnp.int32), lot, side="right")
    return jax.random.permutation(jax.random.fold_in(own_key, 2), count)[grade].astype(jnp.int32)


def deal_out(own_key, own, number, rows, amount, top, limit, lean):
    order = jax.random.permutation(own_key, amount)
    packed, ordinary = shares(amount, rows * top, limit, lean, True), shares(amount, rows * top, limit, lean, False)
    places = jnp.arange(amount)

    def named(sizes, turn):
        used = int((sizes > 0).sum())
        fixed = max(1, used // 4)
        moved = fixed + (places - fixed + turn * (used - fixed)) % max(1, amount - fixed)
        return jnp.zeros((amount,), jnp.int32).at[order[jnp.where(places < fixed, places, moved)]].set(jnp.asarray(sizes, jnp.int32))

    sizes = jnp.where(number % 4 == 0, named(packed, number // 4), named(ordinary, number - number // 4 - 1))
    mixed = jax.random.permutation(jax.random.fold_in(own, 3), amount)
    giver, sink = mixed[0:amount // 2 * 2:2], mixed[1:amount // 2 * 2:2]
    margin = jnp.minimum(sizes[giver] - 1, limit - sizes[sink]) // 2
    margin = jnp.where((giver == order[0]) | (sink == order[0]) | (sizes[sink] == 0), 0, jnp.maximum(margin, 0))
    moved = jax.random.randint(jax.random.fold_in(own, 4), (amount // 2,), 0, 1 << 20) % (margin + 1)
    sizes = sizes.at[giver].add(-moved).at[sink].add(moved)
    members = jnp.searchsorted(jnp.cumsum(sizes), jnp.arange(rows * top), side="right").astype(jnp.int32)
    listing = members.reshape(top, rows).T
    listing = listing[jax.random.permutation(jax.random.fold_in(own, 1), rows)]
    turn = jax.random.randint(jax.random.fold_in(own, 2), (rows, 1), 0, top)
    return jnp.take_along_axis(listing, (jnp.arange(top)[None, :] + turn) % top, axis=1)


def shares(count, total, reach, lean, full):
    loads = [(1 << 20) // math.isqrt(rank ** lean) + 1 for rank in range(1, count + 1)]
    largest = reach if full else min(reach, max(-(-total // count), total * loads[0] // sum(loads)))
    least = 1 if total - largest >= count - 1 else 0
    counts, surplus = [largest] + [least] * (count - 1), total - largest - least * (count - 1)
    while surplus > 0:
        candidates = [i for i in range(1, count) if counts[i] < largest] or [i for i in range(1, count) if counts[i] < reach]
        whole, remaining = sum([loads[i] for i in candidates]), surplus
        for i in candidates:
            more = min(reach - counts[i], max(1, remaining * loads[i] // whole), surplus)
            counts[i] = counts[i] + more
            surplus = surplus - more
    return np.array(counts)


def scatter_about(rng, extent, width, most, shards=(), held_as=jnp.bfloat16):
    entries = width * jax.random.normal(rng, extent, jnp.float32)
    if shards:
        entries = entries * shard_levels(rng, extent, shards, -0.22, 0.18)
    return jnp.clip(entries, -most, most).astype(held_as)


def setup_inputs(seed: int = 0) -> dict:
    key_of = jax.random.split(jax.random.key(seed), 7)
    token_ids = set_ends(ranked_ids(key_of[0], (QUERIES, SEQ), VOCAB, 2), jax.random.fold_in(key_of[0], 3), 0, VOCAB - 1).astype(jnp.int32)
    token_table = scatter_about(key_of[1], (VOCAB, D), 1.0, 6.0, ((0, 32),))
    norm_gain = jnp.clip(1.0 + 0.18 * jax.random.normal(key_of[2], (D,), jnp.float32), 0.1, 1.9)
    slab = scatter_about(key_of[3], (LABELS, D), D ** -0.5, 0.21875, ((0, 32),))
    shortlist_keys = jax.random.split(jax.random.fold_in(key_of[4], 1), QUERIES // GROUP)
    shortlist_turns = jax.random.permutation(jax.random.fold_in(key_of[4], 3), QUERIES // GROUP)
    shortlist = jax.vmap(lambda own, number: deal_out(jax.random.fold_in(key_of[4], 2), own, number, GROUP, NBLK, K, GCAP, 2))(shortlist_keys, shortlist_turns).reshape((QUERIES, K))
    positive_offsets = set_ends(jax.random.randint(key_of[5], (QUERIES, POS), 0, BLOCK), jax.random.fold_in(key_of[5], 1), 0, BLOCK - 1).astype(jnp.int32)
    return dict(token_ids=token_ids, token_table=token_table, norm_gain=norm_gain, slab=slab, shortlist=shortlist, positive_offsets=positive_offsets)


def reference(token_ids, token_table, norm_gain, slab, shortlist, positive_offsets):
    queries = token_ids.shape[0]
    block_rows = math.gcd(queries, 32)
    steps_count = queries // block_rows

    def pool_block(ids_block):
        return lax.optimization_barrier(jnp.sum(jnp.take(token_table, ids_block, axis=0).astype(jnp.float32), axis=1))
    pooled = lax.map(pool_block, token_ids.reshape(steps_count, block_rows, SEQ)).reshape(queries, D) / SEQ
    scale = lax.rsqrt(lax.optimization_barrier(jnp.mean(pooled * pooled, axis=-1, keepdims=True)) + 1e-06)
    embedding = (pooled * scale * norm_gain).astype(jnp.bfloat16)
    label_blocks = slab.reshape(NBLK, BLOCK, D)
    offsets = jnp.concatenate([positive_offsets, jnp.full((queries, K - POS), -1, jnp.int32)], axis=1)
    row_ids = jnp.arange(BLOCK, dtype=jnp.int32)

    def scan_step(totals, inputs):
        embed_rows, list_rows, offset_rows = inputs
        label_rows = jnp.take(label_blocks, list_rows, axis=0).astype(jnp.float32)
        embed_float = embed_rows.astype(jnp.float32)
        logits = jnp.einsum('qkid,qd->qki', label_rows, embed_float)
        target = (offset_rows[:, :, None] == row_ids[None, None, :]).astype(jnp.float32)
        rounded = lax.optimization_barrier((jax.nn.sigmoid(logits) - target).astype(jnp.bfloat16))
        grad_logit = rounded.astype(jnp.float32)
        embed_part = jnp.einsum('qki,qkid->qd', grad_logit, label_rows)
        totals = totals.at[list_rows].add(jnp.einsum('qki,qd->qkid', grad_logit, embed_float))
        return (totals, embed_part)
    grads, embed_parts = lax.scan(scan_step, jnp.zeros((NBLK, BLOCK, D), jnp.float32), (embedding.reshape(steps_count, block_rows, D), shortlist.reshape(steps_count, block_rows, K), offsets.reshape(steps_count, block_rows, K)))
    embed_grad = embed_parts.reshape(queries, D)
    slab_grad = grads.reshape(LABEL_SHARDS, LAB_DEV, D).transpose(1, 0, 2)
    return (embed_grad, slab_grad)
```

```python
import functools

import jax
import jax.numpy as jnp
from jax import lax
from jax.experimental import pallas as pl
from jax.experimental.pallas import tpu as pltpu
from jax.sharding import PartitionSpec as P

K = 8
POS = 2
BLOCK = 128
GCAP = 96
SEQ = 32
NX = 4
NY = 4
NZ = 8
CHIPS = NX * NY
Q_DEV = 64
Q_CHIP = 2 * Q_DEV
GROUP = CHIPS * Q_CHIP
VOC = 952
VOC_PAD = 960
LO = 192
FIELDS = 5
D = 768
BLKS = 16
SLOTS = BLKS * GCAP
HALF = Q_DEV // 2
INFO = 48
MESH = pl.DeviceIdType.MESH
F32 = jnp.float32
BF16 = jnp.bfloat16


def kernel(
    tok_ref, list_ref, pos_ref, gain_ref, table_hbm, slab_hbm,
    eg_ref, sg_ref,
    table, slab, stage, sib_info, my_info, info, lo_ref, w_ref, ct, tmp,
    s_own, s_send, s_recv, r_x, r_y, acc_x, acc_y,
    emb, rank, off2, onehot, slot_off, eslots, hgrad,
    zpart, zsend, zrecv,
    g_send, g_recv, gx_send, gx_recv, gy_recv,
    load_sem, info_s, info_r, pair_s, pair_r, rx_s, rx_r, ry_s, ry_r,
    ex_s, ex_r, ey_s, ey_r, es_s, es_r, z_s, z_r,
    gp_s, gp_r, gx_s, gx_r, gy_s, gy_r,
):
    z = lax.axis_index("dp")
    label = lax.axis_index("label")
    y = lax.div(label, 2 * NX)
    x = lax.rem(lax.div(label, 2), NX)
    c = lax.rem(label, 2)
    o = 1 - c

    def lab(yy, xx, cc):
        return (yy * NX + xx) * 2 + cc

    def at_x(dx):
        return (z, lab(y, lax.rem(x + dx, NX), c))

    def at_y(dy):
        return (z, lab(lax.rem(y + dy, NY), x, c))

    sibling = (z, lab(y, x, o))
    up = (lax.rem(z + 1, NZ), label)
    down = (lax.rem(z + NZ - 1, NZ), label)

    def send(src, dst, ssem, rsem, device):
        copy = pltpu.make_async_remote_copy(
            src_ref=src, dst_ref=dst, send_sem=ssem, recv_sem=rsem,
            device_id=device, device_id_type=MESH,
        )
        copy.start()
        return copy

    load_table = pltpu.make_async_copy(table_hbm, table.at[pl.ds(0, VOC)], load_sem.at[0])
    load_slab = pltpu.make_async_copy(slab_hbm, slab, load_sem.at[1])
    load_table.start()
    load_slab.start()

    barrier = pltpu.get_barrier_semaphore()
    peers = [sibling, up, down] + [at_x(d) for d in (1, 2, 3)] + [at_y(d) for d in (1, 2, 3)]
    for device in peers:
        pl.semaphore_signal(barrier, inc=1, device_id=device, device_id_type=MESH)

    stage[...] = jnp.zeros_like(stage)
    mine_rows = pl.ds(pl.multiple_of(c * Q_DEV, Q_DEV), Q_DEV)
    stage[mine_rows, 0:SEQ] = tok_ref[...]
    stage[mine_rows, SEQ : SEQ + K] = list_ref[...]
    stage[mine_rows, SEQ + K : SEQ + K + POS] = pos_ref[...]
    mine = stage[...].T[0:INFO, :]
    my_info[...] = mine.astype(jnp.int16)
    pl.semaphore_wait(barrier, len(peers))

    pending = []
    first = send(my_info, sib_info, info_s.at[0], info_r.at[0], sibling)
    load_table.wait()
    table[VOC:VOC_PAD, :] = jnp.zeros((VOC_PAD - VOC, D), BF16)
    first.wait()
    info[y, x] = (mine + sib_info[...].astype(jnp.int32)).astype(jnp.int16)
    copies = [
        send(info.at[y, x], info.at[y, x], info_s.at[d], info_r.at[d], at_x(d)) for d in (2, 1, 3)
    ]
    for copy in copies:
        copy.wait()
    copies = [
        send(info.at[y], info.at[y], info_s.at[3 + d], info_r.at[3 + d], at_y(d)) for d in (2, 1, 3)
    ]
    for copy in copies:
        copy.wait()

    base = label * VOC
    half_lo = LO // 2

    def pool_pair(pair, carry):
        for side in range(2):
            j = pair * 2 + side
            ids = info[lax.div(j, NX), lax.rem(j, NX), 0:SEQ, :].astype(jnp.int32) - base
            valid = (ids >= 0) & (ids < VOC)
            high = (ids * 683) >> 17
            weight = jnp.ones_like(ids)
            for f in range(1, FIELDS):
                weight = jnp.where(high == f, 1 << (6 * f), weight)
            lo_ref[...] = jnp.where(valid, ids - high * LO, -1)
            w_ref[...] = jnp.where(valid, weight, 0)
            for part in range(2):
                rows = lax.broadcasted_iota(jnp.int32, (half_lo, 128), 0) + part * half_lo
                acc = jnp.zeros((half_lo, 128), jnp.int32)
                for t in range(SEQ):
                    acc = acc + jnp.where(lo_ref[t : t + 1, :] == rows, w_ref[t : t + 1, :], 0)
                for f in range(FIELDS):
                    field = (acc >> (6 * f)) & 63
                    ct[pl.ds(f * LO + part * half_lo, half_lo), pl.ds(side * 128, 128)] = (
                        field.astype(F32).astype(BF16)
                    )
        pooled = lax.dot_general(
            ct[...], table[...], (((0,), (0,)), ((), ())), preferred_element_type=F32
        )
        tmp[...] = pooled.reshape(4, Q_DEV, D)
        for side in range(2):
            s_own[pair * 2 + side] = tmp[side * 2 + c].reshape(2, HALF, D)
            s_send[pair * 2 + side] = tmp[side * 2 + o].reshape(2, HALF, D)
        at = pl.ds(pair * 2, 2)
        send(s_send.at[at], s_recv.at[at], pair_s.at[pair], pair_r.at[pair], sibling)
        return carry

    lax.fori_loop(0, CHIPS // 2, pool_pair, 0)

    def pair_wait(pair, carry):
        at = pl.ds(pair * 2, 2)
        pltpu.make_async_remote_copy(
            src_ref=s_send.at[at], dst_ref=s_recv.at[at], send_sem=pair_s.at[pair],
            recv_sem=pair_r.at[pair], device_id=sibling, device_id_type=MESH,
        ).wait()
        for side in range(2):
            j = pair * 2 + side
            both = s_own[j] + s_recv[j]
            acc_x[lax.rem(j, NX), lax.div(j, NX)] = both[0]
            acc_y[lax.div(j, NX), lax.rem(j, NX)] = both[1]
        return carry

    lax.fori_loop(0, CHIPS // 2, pair_wait, 0)

    copies_x = {
        d: send(acc_x.at[lax.rem(x + d, NX)], r_x.at[0, d - 1], rx_s.at[0, d - 1], rx_r.at[0, d - 1], at_x(d))
        for d in (2, 1, 3)
    }
    copies_y = {
        d: send(acc_y.at[lax.rem(y + d, NY)], r_x.at[1, d - 1], rx_s.at[1, d - 1], rx_r.at[1, d - 1], at_y(d))
        for d in (2, 1, 3)
    }

    before = (
        lax.broadcasted_iota(jnp.int32, (128, 128), 0) < lax.broadcasted_iota(jnp.int32, (128, 128), 1)
    ).astype(F32).astype(BF16)
    ones = jnp.ones((128, 128), BF16)
    block_ids = lax.broadcasted_iota(jnp.int32, (BLKS, 128), 0) + label * BLKS
    running = jnp.zeros((BLKS, 128), F32)
    for j in range(CHIPS):
        lists = info[j // NX, j % NX, SEQ:INFO, :].astype(jnp.int32)
        hit = jnp.zeros((BLKS, 128), F32)
        place = jnp.zeros((BLKS, 128), F32)
        for k in range(K):
            same = lists[k : k + 1, :] == block_ids
            hit = hit + jnp.where(same, 1.0, 0.0)
            if k < POS:
                at_row = lists[K + k : K + k + 1, :].astype(F32) + 1.0
                place = place + jnp.where(same, at_row, 0.0)
        hit16 = hit.astype(BF16)
        ahead = jnp.dot(hit16, before, preferred_element_type=F32) + running
        running = running + jnp.dot(hit16, ones, preferred_element_type=F32)
        rank[:, j, :] = jnp.where(hit > 0.0, ahead, -1.0)
        off2[:, j, :] = hit + place

    slot_ids = lax.broadcasted_iota(jnp.int32, (GCAP, 128), 0).astype(F32)

    def one_hot(b, carry):
        rows = pl.ds(pl.multiple_of(b * GCAP, GCAP), GCAP)
        found = jnp.zeros((GCAP, 128), F32)
        for j in range(CHIPS):
            lanes = slice(j * 128, (j + 1) * 128)
            same = rank[b, j : j + 1, :] == slot_ids
            onehot[rows, lanes] = jnp.where(same, 1.0, 0.0).astype(BF16)
            found = found + jnp.where(same, off2[b, j : j + 1, :], 0.0)
        slot_off[rows, :] = jnp.broadcast_to(jnp.sum(found, axis=1, keepdims=True), (GCAP, 128))
        return carry

    lax.fori_loop(0, BLKS, one_hot, 0)

    for d in (1, 3, 2):
        copies_x[d].wait()
        copies_y[d].wait()
    acc_x[x] = acc_x[x] + r_x[0, 0] + r_x[0, 1] + r_x[0, 2]
    acc_y[y] = acc_y[y] + r_x[1, 0] + r_x[1, 1] + r_x[1, 2]
    copies = []
    for d in (2, 1, 3):
        yy, xx = lax.rem(y + d, NY), lax.rem(x + d, NX)
        copies.append(send(acc_x.at[x, yy], r_y.at[0, d - 1], ry_s.at[0, d - 1], ry_r.at[0, d - 1], at_y(d)))
        copies.append(send(acc_y.at[y, xx], r_y.at[1, d - 1], ry_s.at[1, d - 1], ry_r.at[1, d - 1], at_x(d)))
    for copy in copies:
        copy.wait()
    gain = gain_ref[...]
    for half in range(2):
        mine_sum = acc_x[x, y] if half == 0 else acc_y[y, x]
        pooled = (mine_sum + r_y[half, 0] + r_y[half, 1] + r_y[half, 2]) / SEQ
        scale = lax.rsqrt(jnp.mean(pooled * pooled, axis=-1, keepdims=True) + 1e-06)
        emb[y, x, c, half] = (pooled * scale * gain).astype(BF16)

    ex = {}
    for d in (2, 1, 3):
        ex[0, d] = send(emb.at[y, x, c, 0], emb.at[y, x, c, 0], ex_s.at[0, d - 1], ex_r.at[0, d - 1], at_x(d))
        ex[1, d] = send(emb.at[y, x, c, 1], emb.at[y, x, c, 1], ex_s.at[1, d - 1], ex_r.at[1, d - 1], at_y(d))
    for d in (1, 3, 2):
        ex[0, d].wait()
        ex[1, d].wait()
    row = emb.at[y, :, c, 0]
    col = emb.at[:, x, c, 1]
    ey = {}
    for d in (2, 1, 3):
        ey[0, d] = send(row, row, ey_s.at[0, d - 1], ey_r.at[0, d - 1], at_y(d))
        ey[1, d] = send(col, col, ey_s.at[1, d - 1], ey_r.at[1, d - 1], at_x(d))
    es = [
        send(row, row, es_s.at[0, 0], es_r.at[0, 0], sibling),
        send(col, col, es_s.at[1, 0], es_r.at[1, 0], sibling),
    ]
    load_slab.wait()
    for d in (1, 3, 2):
        ey[0, d].wait()
        ey[1, d].wait()
        row = emb.at[lax.rem(y + NY - d, NY), :, c, 0]
        col = emb.at[:, lax.rem(x + NX - d, NX), c, 1]
        es.append(send(row, row, es_s.at[0, d], es_r.at[0, d], sibling))
        es.append(send(col, col, es_s.at[1, d], es_r.at[1, d], sibling))
    for copy in es:
        copy.wait()

    def gather_slots(m, carry):
        rows = pl.ds(pl.multiple_of(m * 768, 768), 768)
        eslots[rows, :] = jnp.dot(
            onehot[rows, :], emb[...].reshape(GROUP, D), preferred_element_type=F32
        ).astype(BF16)
        return carry

    lax.fori_loop(0, SLOTS // 768, gather_slots, 0)

    pair_rows = 2 * GCAP
    row_ids = lax.broadcasted_iota(jnp.int32, (pair_rows, 2 * BLOCK), 0)
    col_ids = lax.broadcasted_iota(jnp.int32, (pair_rows, 2 * BLOCK), 1)
    same_block = (row_ids >= GCAP) == (col_ids >= BLOCK)
    col_in = jnp.where(col_ids >= BLOCK, col_ids - BLOCK, col_ids).astype(F32) + 2.0

    def grads(offset):
        dest = lax.rem(z + offset + NZ, NZ)
        srows = pl.ds(pl.multiple_of(dest * pair_rows, pair_rows), pair_rows)
        lrows = pl.ds(pl.multiple_of(dest * 2 * BLOCK, 2 * BLOCK), 2 * BLOCK)
        es_rows = eslots[srows, :]
        labels = slab[lrows, :]
        logits = lax.dot_general(es_rows, labels, (((1,), (1,)), ((), ())), preferred_element_type=F32)
        seen = slot_off[srows, :]
        seen = jnp.concatenate([seen, seen], axis=1)
        g = jax.nn.sigmoid(logits) - jnp.where(seen == col_in, 1.0, 0.0)
        g = jnp.where(same_block & (seen > 0.0), g, 0.0).astype(BF16)
        hgrad[srows, :] = jnp.dot(g, labels, preferred_element_type=F32).astype(BF16)
        return lax.dot_general(g, es_rows, (((0,), (0,)), ((), ())), preferred_element_type=F32)

    zc = {}

    def z_send(way, step, sub):
        zc[way, step, sub] = send(
            zsend.at[way, step, sub], zrecv.at[way, step, sub],
            z_s.at[way, step, sub], z_r.at[way, step, sub], up if way == 0 else down,
        )

    def z_fill(way, step, sub, with_recv):
        value = zpart[way, step - 1, pl.ds(sub * BLOCK, BLOCK), :]
        if with_recv:
            value = value + zrecv[way, step - 1, sub].astype(F32)
        zsend[way, step, sub] = value.astype(BF16)
        z_send(way, step, sub)

    far = grads(4)
    for way in range(2):
        zsend[way, 0, way] = far[way * BLOCK : (way + 1) * BLOCK, :].astype(BF16)
        z_send(way, 0, way)
    for way, sign in ((0, 1), (1, -1)):
        zpart[way, 0] = grads(3 * sign)
        z_fill(way, 1, 1 - way, False)
    for way in range(2):
        zc[way, 0, way].wait()
        z_fill(way, 1, way, True)
    for step in (2, 3):
        for way, sign in ((0, 1), (1, -1)):
            zpart[way, step - 1] = grads((4 - step) * sign)
    own_part = grads(0)
    sg_ref[...] = own_part
    for way in range(2):
        zc[way, 1, 1 - way].wait()
        z_fill(way, 2, 1 - way, True)
    for way in range(2):
        zc[way, 1, way].wait()
        z_fill(way, 2, way, True)

    def spread_pair(pair, carry):
        lanes = pl.ds(pl.multiple_of(pair * 256, 256), 256)
        grad = lax.dot_general(
            onehot[:, lanes], hgrad[...], (((0,), (0,)), ((), ())), preferred_element_type=F32
        )
        tmp[...] = grad.reshape(4, Q_DEV, D)
        for side in range(2):
            s_own[pair * 2 + side] = tmp[side * 2 + c].reshape(2, HALF, D)
            g_send[pair * 2 + side] = tmp[side * 2 + o].astype(BF16)
        at = pl.ds(pair * 2, 2)
        send(g_send.at[at], g_recv.at[at], gp_s.at[pair], gp_r.at[pair], sibling)
        return carry

    lax.fori_loop(0, CHIPS // 2, spread_pair, 0)

    for sub_of in (1, 0):
        for way in range(2):
            sub = 1 - way if sub_of else way
            zc[way, 2, sub].wait()
            z_fill(way, 3, sub, True)

    def grad_pair_wait(pair, carry):
        at = pl.ds(pair * 2, 2)
        pltpu.make_async_remote_copy(
            src_ref=g_send.at[at], dst_ref=g_recv.at[at], send_sem=gp_s.at[pair],
            recv_sem=gp_r.at[pair], device_id=sibling, device_id_type=MESH,
        ).wait()
        for side in range(2):
            j = pair * 2 + side
            both = s_own[j] + g_recv[j].astype(F32).reshape(2, HALF, D)
            xx, yy = lax.rem(j, NX), lax.div(j, NX)
            acc_x[xx, yy] = both[0]
            acc_y[yy, xx] = both[1]
            gx_send[0, xx, yy] = both[0].astype(BF16)
            gx_send[1, yy, xx] = both[1].astype(BF16)
        return carry

    lax.fori_loop(0, CHIPS // 2, grad_pair_wait, 0)

    copies = []
    for d in (2, 1, 3):
        copies.append(send(gx_send.at[0, lax.rem(x + d, NX)], gx_recv.at[0, d - 1], gx_s.at[0, d - 1], gx_r.at[0, d - 1], at_x(d)))
        copies.append(send(gx_send.at[1, lax.rem(y + d, NY)], gx_recv.at[1, d - 1], gx_s.at[1, d - 1], gx_r.at[1, d - 1], at_y(d)))
    for copy in copies:
        copy.wait()
    acc_x[x] = acc_x[x] + sum(gx_recv[0, i].astype(F32) for i in range(3))
    acc_y[y] = acc_y[y] + sum(gx_recv[1, i].astype(F32) for i in range(3))
    copies = []
    for d in (2, 1, 3):
        yy, xx = lax.rem(y + d, NY), lax.rem(x + d, NX)
        copies.append(send(acc_x.at[x, yy], gy_recv.at[0, d - 1], gy_s.at[0, d - 1], gy_r.at[0, d - 1], at_y(d)))
        copies.append(send(acc_y.at[y, xx], gy_recv.at[1, d - 1], gy_s.at[1, d - 1], gy_r.at[1, d - 1], at_x(d)))
    for sub in range(2):
        rows = pl.ds(sub * BLOCK, BLOCK)
        for way in range(2):
            zc[way, 3, sub].wait()
        sg_ref[rows, :] = sg_ref[rows, :] + zrecv[0, 3, sub].astype(F32) + zrecv[1, 3, sub].astype(F32)
    for copy in copies:
        copy.wait()
    eg_ref[0:HALF, :] = acc_x[x, y] + gy_recv[0, 0] + gy_recv[0, 1] + gy_recv[0, 2]
    eg_ref[HALF:Q_DEV, :] = acc_y[y, x] + gy_recv[1, 0] + gy_recv[1, 1] + gy_recv[1, 2]


def local(token_ids, token_table, norm_gain, slab, shortlist, positive_offsets):
    vmem = pl.BlockSpec(memory_space=pltpu.VMEM)
    anyspace = pl.BlockSpec(memory_space=pl.ANY)
    dma = pltpu.SemaphoreType.DMA
    scratch = dict(
        table=pltpu.VMEM((VOC_PAD, D), BF16),
        slab=pltpu.VMEM((BLKS * BLOCK, D), BF16),
        stage=pltpu.VMEM((128, 128), jnp.int32),
        sib_info=pltpu.VMEM((INFO, 128), jnp.int16),
        my_info=pltpu.VMEM((INFO, 128), jnp.int16),
        info=pltpu.VMEM((NY, NX, INFO, 128), jnp.int16),
        lo_ref=pltpu.VMEM((SEQ, 128), jnp.int32),
        w_ref=pltpu.VMEM((SEQ, 128), jnp.int32),
        ct=pltpu.VMEM((VOC_PAD, 256), BF16),
        tmp=pltpu.VMEM((4, Q_DEV, D), F32),
        s_own=pltpu.VMEM((CHIPS, 2, HALF, D), F32),
        s_send=pltpu.VMEM((CHIPS, 2, HALF, D), F32),
        s_recv=pltpu.VMEM((CHIPS, 2, HALF, D), F32),
        r_x=pltpu.VMEM((2, 3, NY, HALF, D), F32),
        r_y=pltpu.VMEM((2, 3, HALF, D), F32),
        acc_x=pltpu.VMEM((NX, NY, HALF, D), F32),
        acc_y=pltpu.VMEM((NY, NX, HALF, D), F32),
        emb=pltpu.VMEM((NY, NX, 2, 2, HALF, D), BF16),
        rank=pltpu.VMEM((BLKS, CHIPS, 128), F32),
        off2=pltpu.VMEM((BLKS, CHIPS, 128), F32),
        onehot=pltpu.VMEM((SLOTS, GROUP), BF16),
        slot_off=pltpu.VMEM((SLOTS, 128), F32),
        eslots=pltpu.VMEM((SLOTS, D), BF16),
        hgrad=pltpu.VMEM((SLOTS, D), BF16),
        zpart=pltpu.VMEM((2, 3, 2 * BLOCK, D), F32),
        zsend=pltpu.VMEM((2, 4, 2, BLOCK, D), BF16),
        zrecv=pltpu.VMEM((2, 4, 2, BLOCK, D), BF16),
        g_send=pltpu.VMEM((CHIPS, Q_DEV, D), BF16),
        g_recv=pltpu.VMEM((CHIPS, Q_DEV, D), BF16),
        gx_send=pltpu.VMEM((2, 4, 4, HALF, D), BF16),
        gx_recv=pltpu.VMEM((2, 3, 4, HALF, D), BF16),
        gy_recv=pltpu.VMEM((2, 3, HALF, D), F32),
        load_sem=dma((2,)),
        info_s=dma((7,)), info_r=dma((7,)),
        pair_s=dma((CHIPS // 2,)), pair_r=dma((CHIPS // 2,)),
        rx_s=dma((2, 3)), rx_r=dma((2, 3)), ry_s=dma((2, 3)), ry_r=dma((2, 3)),
        ex_s=dma((2, 3)), ex_r=dma((2, 3)), ey_s=dma((2, 3)), ey_r=dma((2, 3)),
        es_s=dma((2, 4)), es_r=dma((2, 4)),
        z_s=dma((2, 4, 2)), z_r=dma((2, 4, 2)),
        gp_s=dma((CHIPS // 2,)), gp_r=dma((CHIPS // 2,)),
        gx_s=dma((2, 3)), gx_r=dma((2, 3)), gy_s=dma((2, 3)), gy_r=dma((2, 3)),
    )
    eg, sg = pl.pallas_call(
        kernel,
        out_shape=(
            jax.ShapeDtypeStruct((Q_DEV, D), F32),
            jax.ShapeDtypeStruct((2 * BLOCK, D), F32),
        ),
        in_specs=[vmem, vmem, vmem, vmem, anyspace, anyspace],
        out_specs=(vmem, vmem),
        scratch_shapes=list(scratch.values()),
        compiler_params=pltpu.CompilerParams(
            collective_id=0, has_side_effects=True, vmem_limit_bytes=63 << 20
        ),
    )(token_ids, shortlist, positive_offsets, norm_gain.reshape(1, D), token_table, slab)
    return eg, sg.reshape(2 * BLOCK, 1, D)


def solution(mesh):
    return jax.shard_map(
        local,
        mesh=mesh,
        in_specs=(
            P(("dp", "label"), None),
            P("label", None),
            P(),
            P("label", None),
            P(("dp", "label"), None),
            P(("dp", "label"), None),
        ),
        out_specs=(P(("dp", "label"), None), P("dp", "label", None)),
        check_vma=False,
    )
```

```python
import math

import jax
import jax.numpy as jnp
from jax import lax
from jax.experimental import pallas as pl
from jax.experimental.pallas import tpu as pltpu
from jax.sharding import PartitionSpec as P

K = 8
POS = 2
BLOCK = 128
GCAP = 96
SEQ = 32
NX = 4
NY = 4
NZ = 8
CHIPS = NX * NY
Q_DEV = 64
Q_CHIP = 2 * Q_DEV
GROUP = CHIPS * Q_CHIP
VOC = 952
VOC_PAD = 960
LO = 192
FIELDS = 5
D = 768
BLKS = 16
SLOTS = BLKS * GCAP
HALF = Q_DEV // 2
INFO = 48
TILES = 8
TILE = 256
Q_COLS = D + 128
TOP = 32000.0
MESH = pl.DeviceIdType.MESH
F32 = jnp.float32
BF16 = jnp.bfloat16


def pack_rows(value, dst):
    largest = jnp.max(jnp.abs(value), axis=-1, keepdims=True)
    step = jnp.ceil(jnp.log(jnp.maximum(largest, 1e-30)) * (8.0 / math.log(2.0)))
    factor = jnp.exp(step * (-math.log(2.0) / 8.0)) * TOP
    dst[:, 0:D] = jnp.round(value * factor).astype(jnp.int32).astype(jnp.int16)
    dst[:, D:Q_COLS] = jnp.broadcast_to(step, (value.shape[0], 128)).astype(jnp.int32).astype(jnp.int16)


def unpack_rows(src):
    step = src[:, D : D + 1].astype(jnp.int32).astype(F32)
    factor = jnp.exp(step * (math.log(2.0) / 8.0)) * (1.0 / TOP)
    return src[:, 0:D].astype(jnp.int32).astype(F32) * factor


def kernel(
    tok_ref, list_ref, pos_ref, gain_ref, table_hbm, slab_hbm,
    eg_ref, sg_ref,
    table, slab, stage, sib_info, my_info, info, lo_ref, w_ref, ct, tmp,
    s_own, s_send, s_recv, qa, ra, qb, rb, qa2, ra2, qb2, rb2, acc_a, acc_b,
    emb, rank, off2, onehot, slot_off, eacc, eslots, hgrad,
    zpart, zsend, zrecv,
    g_own, g_send, g_recv, gx_send, gx_recv, gy_send, gy_recv,
    load_sem, info_s, info_r, pair_s, pair_r, ra_s, ra_r, rb_s, rb_r, r2_s, r2_r,
    ex_s, ex_r, ey_s, ey_r, es_s, es_r, z_s, z_r,
    gp_s, gp_r, gx_s, gx_r, gy_s, gy_r,
):
    z = lax.axis_index("dp")
    label = lax.axis_index("label")
    y = lax.div(label, 2 * NX)
    x = lax.rem(lax.div(label, 2), NX)
    c = lax.rem(label, 2)
    o = 1 - c

    def lab(yy, xx, cc):
        return (yy * NX + xx) * 2 + cc

    def at_x(dx):
        return (z, lab(y, lax.rem(x + dx, NX), c))

    def at_y(dy):
        return (z, lab(lax.rem(y + dy, NY), x, c))

    sibling = (z, lab(y, x, o))
    up = (lax.rem(z + 1, NZ), label)
    down = (lax.rem(z + NZ - 1, NZ), label)

    def send(src, dst, ssem, rsem, device):
        copy = pltpu.make_async_remote_copy(
            src_ref=src, dst_ref=dst, send_sem=ssem, recv_sem=rsem,
            device_id=device, device_id_type=MESH,
        )
        copy.start()
        return copy

    load_table = pltpu.make_async_copy(table_hbm, table.at[pl.ds(0, VOC)], load_sem.at[0])
    load_slab = pltpu.make_async_copy(slab_hbm, slab, load_sem.at[1])
    load_table.start()
    load_slab.start()

    barrier = pltpu.get_barrier_semaphore()
    peers = [sibling, up, down] + [at_x(d) for d in (1, 2, 3)] + [at_y(d) for d in (1, 2, 3)]
    for device in peers:
        pl.semaphore_signal(barrier, inc=1, device_id=device, device_id_type=MESH)

    stage[...] = jnp.zeros_like(stage)
    for core in range(2):

        @pl.when(c == core)
        def _():
            for half in range(2):
                src = slice(half * HALF, (half + 1) * HALF)
                dst = slice(half * Q_DEV + core * HALF, half * Q_DEV + (core + 1) * HALF)
                stage[0:SEQ, dst] = tok_ref[:, src]
                stage[SEQ : SEQ + K, dst] = list_ref[:, src]
                stage[SEQ + K : SEQ + K + POS, dst] = pos_ref[:, src]

    mine = stage[...]
    my_info[...] = mine.astype(jnp.int16)
    pl.semaphore_wait(barrier, len(peers))

    first = send(my_info, sib_info, info_s.at[0], info_r.at[0], sibling)
    load_table.wait()
    table[VOC:VOC_PAD, :] = jnp.zeros((VOC_PAD - VOC, D), BF16)
    first.wait()
    info[y, x] = (mine + sib_info[...].astype(jnp.int32)).astype(jnp.int16)
    copies = [
        send(info.at[y, x], info.at[y, x], info_s.at[d], info_r.at[d], at_x(d)) for d in (2, 1, 3)
    ]
    for copy in copies:
        copy.wait()
    info_y = {
        d: send(info.at[y], info.at[y], info_s.at[3 + d], info_r.at[3 + d], at_y(d)) for d in (2, 1, 3)
    }

    base = label * VOC
    half_lo = LO // 2
    row_steps = (0, 2, 1, 3)
    pair_copies = {}
    ra_copies, rb_copies = {}, {}

    def pool_row(i):
        r = lax.rem(y + row_steps[i], NY)

        def pool_pair(pair, carry):
            for side in range(2):
                ids = info[r, pair * 2 + side, 0:SEQ, :].astype(jnp.int32) - base
                valid = (ids >= 0) & (ids < VOC)
                high = (ids * 683) >> 17
                weight = jnp.ones_like(ids)
                for f in range(1, FIELDS):
                    weight = jnp.where(high == f, 1 << (6 * f), weight)
                lo_ref[...] = jnp.where(valid, ids - high * LO, -1)
                w_ref[...] = jnp.where(valid, weight, 0)
                for part in range(2):
                    rows = lax.broadcasted_iota(jnp.int32, (half_lo, 128), 0) + part * half_lo
                    acc = jnp.zeros((half_lo, 128), jnp.int32)
                    for t in range(SEQ):
                        acc = acc + jnp.where(lo_ref[t : t + 1, :] == rows, w_ref[t : t + 1, :], 0)
                    for f in range(FIELDS):
                        field = (acc >> (6 * f)) & 63
                        ct[pl.ds(f * LO + part * half_lo, half_lo), pl.ds(side * 128, 128)] = (
                            field.astype(F32).astype(BF16)
                        )
            pooled = lax.dot_general(
                ct[...], table[...], (((0,), (0,)), ((), ())), preferred_element_type=F32
            )
            tmp[...] = pooled.reshape(4, 2, HALF, D)
            for side in range(2):
                for half in range(2):
                    s_own[i, pair * 2 + side, half] = tmp[side * 2 + half, c]
                    s_send[i, pair * 2 + side, half] = tmp[side * 2 + half, o]
            at = pl.ds(pair * 2, 2)
            send(s_send.at[i, at], s_recv.at[i, at], pair_s.at[i, pair], pair_r.at[i, pair], sibling)
            return carry

        lax.fori_loop(0, NX // 2, pool_pair, 0)

    def finish_row(i):
        for pair in range(NX // 2):
            at = pl.ds(pair * 2, 2)
            pltpu.make_async_remote_copy(
                src_ref=s_send.at[i, at], dst_ref=s_recv.at[i, at], send_sem=pair_s.at[i, pair],
                recv_sem=pair_r.at[i, pair], device_id=sibling, device_id_type=MESH,
            ).wait()
        for d in (2, 1, 3, 0):
            xx = lax.rem(x + d, NX)
            both = s_own[i, xx, 0] + s_recv[i, xx, 0]
            if d == 0:
                acc_a[i] = both
            else:
                pack_rows(both, qa.at[i, d - 1])
                ra_copies[i, d] = send(
                    qa.at[i, d - 1], ra.at[i, d - 1], ra_s.at[i, d - 1], ra_r.at[i, d - 1], at_x(d)
                )
        for d in range(NX):
            xx = lax.rem(x + d, NX)
            both = s_own[i, xx, 1] + s_recv[i, xx, 1]
            if i == 0:
                acc_b[d] = both
            else:
                pack_rows(both, qb.at[i - 1, d])
        if i:
            rb_copies[i] = send(
                qb.at[i - 1], rb.at[i - 1], rb_s.at[i - 1], rb_r.at[i - 1], at_y(row_steps[i])
            )

    pool_row(0)
    for i in range(1, NY):
        info_y[NY - row_steps[i]].wait()
        pool_row(i)
        finish_row(i - 1)
    finish_row(NY - 1)

    before = (
        lax.broadcasted_iota(jnp.int32, (128, 128), 0) < lax.broadcasted_iota(jnp.int32, (128, 128), 1)
    ).astype(F32).astype(BF16)
    ones = jnp.ones((128, 128), BF16)
    block_ids = lax.broadcasted_iota(jnp.int32, (BLKS, 128), 0) + label * BLKS
    low_lanes = lax.broadcasted_iota(jnp.int32, (INFO - SEQ, 128), 1) < Q_DEV
    running = jnp.zeros((BLKS, 128), F32)
    for j in range(2 * TILES):
        tile, p = j // 2, j % 2
        if tile < NY:
            left = info[tile, 2 * p, SEQ:INFO, :].astype(jnp.int32)
            right = info[tile, 2 * p + 1, SEQ:INFO, :].astype(jnp.int32)
            lists = jnp.where(low_lanes, left, pltpu.roll(right, Q_DEV, 1))
        else:
            left = info[2 * p, tile - NY, SEQ:INFO, :].astype(jnp.int32)
            right = info[2 * p + 1, tile - NY, SEQ:INFO, :].astype(jnp.int32)
            lists = jnp.where(low_lanes, pltpu.roll(left, Q_DEV, 1), right)
        hit = jnp.zeros((BLKS, 128), F32)
        place = jnp.zeros((BLKS, 128), F32)
        for k in range(K):
            same = lists[k : k + 1, :] == block_ids
            hit = hit + jnp.where(same, 1.0, 0.0)
            if k < POS:
                at_row = lists[K + k : K + k + 1, :].astype(F32) + 1.0
                place = place + jnp.where(same, at_row, 0.0)
        hit16 = hit.astype(BF16)
        ahead = jnp.dot(hit16, before, preferred_element_type=F32) + running
        running = running + jnp.dot(hit16, ones, preferred_element_type=F32)
        rank[:, j, :] = jnp.where(hit > 0.0, ahead, -1.0)
        off2[:, j, :] = hit + place

    slot_ids = lax.broadcasted_iota(jnp.int32, (GCAP, 128), 0).astype(F32)

    def one_hot(b, carry):
        rows = pl.ds(pl.multiple_of(b * GCAP, GCAP), GCAP)
        found = jnp.zeros((GCAP, 128), F32)
        for j in range(2 * TILES):
            lanes = slice((j % 2) * 128, (j % 2 + 1) * 128)
            same = rank[b, j : j + 1, :] == slot_ids
            onehot[j // 2, rows, lanes] = jnp.where(same, 1.0, 0.0).astype(BF16)
            found = found + jnp.where(same, off2[b, j : j + 1, :], 0.0)
        slot_off[rows, :] = jnp.broadcast_to(jnp.sum(found, axis=1, keepdims=True), (GCAP, 128))
        return carry

    lax.fori_loop(0, BLKS, one_hot, 0)

    second = []
    for i in (1, 2, 3, 0):
        total = acc_a[i]
        for d in (1, 3, 2):
            ra_copies[i, d].wait()
            total = total + unpack_rows(ra.at[i, d - 1])
        if i:
            pack_rows(total, qa2.at[i - 1])
            second.append(
                send(qa2.at[i - 1], ra2.at[i - 1], r2_s.at[0, i - 1], r2_r.at[0, i - 1], at_y(row_steps[i]))
            )
        else:
            acc_a[0] = total
    for i in (1, 2, 3):
        rb_copies[i].wait()
    for d in (2, 1, 3, 0):
        total = acc_b[d]
        for i in range(3):
            total = total + unpack_rows(rb.at[i, d])
        if d:
            pack_rows(total, qb2.at[d - 1])
            second.append(
                send(qb2.at[d - 1], rb2.at[d - 1], r2_s.at[1, d - 1], r2_r.at[1, d - 1], at_x(d))
            )
        else:
            acc_b[0] = total
    for copy in second:
        copy.wait()
    gain = gain_ref[...].reshape(1, D)
    for half in range(2):
        pooled = acc_a[0] if half == 0 else acc_b[0]
        for i in range(3):
            pooled = pooled + unpack_rows(ra2.at[i] if half == 0 else rb2.at[i])
        pooled = pooled / SEQ
        scale = lax.rsqrt(jnp.mean(pooled * pooled, axis=-1, keepdims=True) + 1e-06)
        value = (pooled * scale * gain).astype(BF16)
        if half == 0:
            emb[y, x, c] = value
        else:
            emb[NY + x, y, c] = value

    mine_a, mine_b = emb.at[y, x, c], emb.at[NY + x, y, c]
    ex = {}
    for d in (2, 1, 3):
        ex[0, d] = send(mine_a, mine_a, ex_s.at[0, d - 1], ex_r.at[0, d - 1], at_x(d))
        ex[1, d] = send(mine_b, mine_b, ex_s.at[1, d - 1], ex_r.at[1, d - 1], at_y(d))
    for d in (1, 3, 2):
        ex[0, d].wait()
        ex[1, d].wait()
    row, col = emb.at[y, :, c], emb.at[NY + x, :, c]
    ey = {}
    for d in (2, 1, 3):
        ey[0, d] = send(row, row, ey_s.at[0, d - 1], ey_r.at[0, d - 1], at_y(d))
        ey[1, d] = send(col, col, ey_s.at[1, d - 1], ey_r.at[1, d - 1], at_x(d))

    def forward(d):
        row = emb.at[lax.rem(y + NY - d, NY), :, c]
        col = emb.at[NY + lax.rem(x + NX - d, NX), :, c]
        return [
            send(row, row, es_s.at[0, d], es_r.at[0, d], sibling),
            send(col, col, es_s.at[1, d], es_r.at[1, d], sibling),
        ]

    chunk = SLOTS // 4

    def gather_slots(d, kind):
        tile_a = lax.rem(y + NY - d, NY)
        tile_b = NY + lax.rem(x + NX - d, NX)

        def body(m, carry):
            rows = pl.ds(pl.multiple_of(m * chunk, chunk), chunk)
            value = jnp.dot(
                onehot[tile_a, rows, :], emb[tile_a].reshape(TILE, D), preferred_element_type=F32
            ) + jnp.dot(onehot[tile_b, rows, :], emb[tile_b].reshape(TILE, D), preferred_element_type=F32)
            if kind:
                value = value + eacc[rows, :]
            if kind == 2:
                eslots[rows, :] = value.astype(BF16)
            else:
                eacc[rows, :] = value
            return carry

        lax.fori_loop(0, SLOTS // chunk, body, 0)

    moving = forward(0)
    for n, d in enumerate((1, 3, 2, None)):
        for copy in moving:
            copy.wait()
        if d is not None:
            for half in range(2):
                ey[half, d].wait()
            moving = forward(d)
        gather_slots((0, 1, 3, 2)[n], 0 if n == 0 else 2 if n == 3 else 1)
    load_slab.wait()

    pair_rows = 2 * GCAP
    row_ids = lax.broadcasted_iota(jnp.int32, (pair_rows, 2 * BLOCK), 0)
    col_ids = lax.broadcasted_iota(jnp.int32, (pair_rows, 2 * BLOCK), 1)
    same_block = (row_ids >= GCAP) == (col_ids >= BLOCK)
    col_in = jnp.where(col_ids >= BLOCK, col_ids - BLOCK, col_ids).astype(F32) + 2.0

    def grads(offset):
        dest = lax.rem(z + offset + NZ, NZ)
        srows = pl.ds(pl.multiple_of(dest * pair_rows, pair_rows), pair_rows)
        lrows = pl.ds(pl.multiple_of(dest * 2 * BLOCK, 2 * BLOCK), 2 * BLOCK)
        es_rows = eslots[srows, :]
        labels = slab[lrows, :]
        logits = lax.dot_general(es_rows, labels, (((1,), (1,)), ((), ())), preferred_element_type=F32)
        seen = slot_off[srows, :]
        seen = jnp.concatenate([seen, seen], axis=1)
        g = jax.nn.sigmoid(logits) - jnp.where(seen == col_in, 1.0, 0.0)
        g = jnp.where(same_block & (seen > 0.0), g, 0.0).astype(BF16)
        hgrad[srows, :] = jnp.dot(g, labels, preferred_element_type=F32).astype(BF16)
        return lax.dot_general(g, es_rows, (((0,), (0,)), ((), ())), preferred_element_type=F32)

    zc = {}

    def z_send(way, step, sub):
        zc[way, step, sub] = send(
            zsend.at[way, step, sub], zrecv.at[way, step, sub],
            z_s.at[way, step, sub], z_r.at[way, step, sub], up if way == 0 else down,
        )

    def z_fill(way, step, sub, with_recv):
        value = zpart[way, step - 1, pl.ds(sub * BLOCK, BLOCK), :]
        if with_recv:
            value = value + zrecv[way, step - 1, sub].astype(F32)
        zsend[way, step, sub] = value.astype(BF16)
        z_send(way, step, sub)

    def z_pass(step, first):
        for way in range(2):
            sub = 1 - way if first else way
            zc[way, step - 1, sub].wait()
            z_fill(way, step, sub, True)

    far = grads(4)
    for way in range(2):
        zsend[way, 0, way] = far[way * BLOCK : (way + 1) * BLOCK, :].astype(BF16)
        z_send(way, 0, way)
    for way, sign in ((0, 1), (1, -1)):
        zpart[way, 0] = grads(3 * sign)
        z_fill(way, 1, 1 - way, False)
    for step in (2, 3):
        for way, sign in ((0, 1), (1, -1)):
            zpart[way, step - 1] = grads((4 - step) * sign)
    sg_ref[...] = grads(0)
    z_pass(1, False)

    def spread(tiles):
        def body(k, carry):
            grad = lax.dot_general(
                onehot[k], hgrad[...], (((0,), (0,)), ((), ())), preferred_element_type=F32
            )
            tmp[...] = grad.reshape(4, 2, HALF, D)
            for side in range(4):
                g_own[k, side] = tmp[side, c]
                g_send[k, side] = tmp[side, o].astype(BF16)
            send(g_send.at[k], g_recv.at[k], gp_s.at[k], gp_r.at[k], sibling)
            return carry

        lax.fori_loop(tiles[0], tiles[1], body, 0)

    gx = {}

    def to_chips(k):
        pltpu.make_async_remote_copy(
            src_ref=g_send.at[k], dst_ref=g_recv.at[k], send_sem=gp_s.at[k],
            recv_sem=gp_r.at[k], device_id=sibling, device_id_type=MESH,
        ).wait()
        for d in (2, 1, 3, 0):
            if k < NY:
                piece, device = lax.rem(x + d, NX), at_x(d)
            else:
                piece, device = lax.rem(y + d, NY), at_y(d)
            both = g_own[k, piece] + g_recv[k, piece].astype(F32)
            if d == 0:
                g_own[k, 0] = both
            else:
                gx_send[k, d - 1] = both.astype(BF16)
                gx[k, d] = send(
                    gx_send.at[k, d - 1], gx_recv.at[k, d - 1], gx_s.at[k, d - 1], gx_r.at[k, d - 1], device
                )

    spread((0, 2))
    spread((4, 6))
    z_pass(2, True)
    for k in (0, 4, 1, 5):
        to_chips(k)
    spread((2, 4))
    spread((6, 8))
    z_pass(2, False)
    for k in (2, 6, 3, 7):
        to_chips(k)
    z_pass(3, True)

    def own_total(k):
        total = g_own[k, 0]
        for d in (1, 3, 2):
            total = total + gx_recv[k, d - 1].astype(F32)
        return total

    for k in range(TILES):
        for d in (1, 3, 2):
            gx[k, d].wait()
    z_pass(3, False)
    copies = []
    for d in (2, 1, 3):
        gy_send[0, d - 1] = own_total(lax.rem(y + d, NY))
        copies.append(send(gy_send.at[0, d - 1], gy_recv.at[0, d - 1], gy_s.at[0, d - 1], gy_r.at[0, d - 1], at_y(d)))
        gy_send[1, d - 1] = own_total(NY + lax.rem(x + d, NX))
        copies.append(send(gy_send.at[1, d - 1], gy_recv.at[1, d - 1], gy_s.at[1, d - 1], gy_r.at[1, d - 1], at_x(d)))
    eg_ref[0:HALF, :] = own_total(y)
    eg_ref[HALF:Q_DEV, :] = own_total(NY + x)
    for copy in copies:
        copy.wait()
    for half in range(2):
        rows = pl.ds(half * HALF, HALF)
        eg_ref[rows, :] = eg_ref[rows, :] + gy_recv[half, 0] + gy_recv[half, 1] + gy_recv[half, 2]
    for first in (True, False):
        for way in range(2):
            sub = 1 - way if first else way
            zc[way, 3, sub].wait()
            rows = pl.ds(sub * BLOCK, BLOCK)
            sg_ref[rows, :] = sg_ref[rows, :] + zrecv[way, 3, sub].astype(F32)


def local(token_ids, token_table, norm_gain, slab, shortlist, positive_offsets):
    vmem = pl.BlockSpec(memory_space=pltpu.VMEM)
    anyspace = pl.BlockSpec(memory_space=pl.ANY)
    dma = pltpu.SemaphoreType.DMA
    i16 = jnp.int16
    scratch = dict(
        table=pltpu.VMEM((VOC_PAD, D), BF16),
        slab=pltpu.VMEM((BLKS * BLOCK, D), BF16),
        stage=pltpu.VMEM((INFO, 128), jnp.int32),
        sib_info=pltpu.VMEM((INFO, 128), i16),
        my_info=pltpu.VMEM((INFO, 128), i16),
        info=pltpu.VMEM((NY, NX, INFO, 128), i16),
        lo_ref=pltpu.VMEM((SEQ, 128), jnp.int32),
        w_ref=pltpu.VMEM((SEQ, 128), jnp.int32),
        ct=pltpu.VMEM((VOC_PAD, 256), BF16),
        tmp=pltpu.VMEM((4, 2, HALF, D), F32),
        s_own=pltpu.VMEM((NY, NX, 2, HALF, D), F32),
        s_send=pltpu.VMEM((NY, NX, 2, HALF, D), F32),
        s_recv=pltpu.VMEM((NY, NX, 2, HALF, D), F32),
        qa=pltpu.VMEM((NY, 3, HALF, Q_COLS), i16),
        ra=pltpu.VMEM((NY, 3, HALF, Q_COLS), i16),
        qb=pltpu.VMEM((3, NX, HALF, Q_COLS), i16),
        rb=pltpu.VMEM((3, NX, HALF, Q_COLS), i16),
        qa2=pltpu.VMEM((3, HALF, Q_COLS), i16),
        ra2=pltpu.VMEM((3, HALF, Q_COLS), i16),
        qb2=pltpu.VMEM((3, HALF, Q_COLS), i16),
        rb2=pltpu.VMEM((3, HALF, Q_COLS), i16),
        acc_a=pltpu.VMEM((NY, HALF, D), F32),
        acc_b=pltpu.VMEM((NX, HALF, D), F32),
        emb=pltpu.VMEM((TILES, 4, 2, HALF, D), BF16),
        rank=pltpu.VMEM((BLKS, 2 * TILES, 128), F32),
        off2=pltpu.VMEM((BLKS, 2 * TILES, 128), F32),
        onehot=pltpu.VMEM((TILES, SLOTS, TILE), BF16),
        slot_off=pltpu.VMEM((SLOTS, 128), F32),
        eacc=pltpu.VMEM((SLOTS, D), F32),
        eslots=pltpu.VMEM((SLOTS, D), BF16),
        hgrad=pltpu.VMEM((SLOTS, D), BF16),
        zpart=pltpu.VMEM((2, 3, 2 * BLOCK, D), F32),
        zsend=pltpu.VMEM((2, 4, 2, BLOCK, D), BF16),
        zrecv=pltpu.VMEM((2, 4, 2, BLOCK, D), BF16),
        g_own=pltpu.VMEM((TILES, 4, HALF, D), F32),
        g_send=pltpu.VMEM((TILES, 4, HALF, D), BF16),
        g_recv=pltpu.VMEM((TILES, 4, HALF, D), BF16),
        gx_send=pltpu.VMEM((TILES, 3, HALF, D), BF16),
        gx_recv=pltpu.VMEM((TILES, 3, HALF, D), BF16),
        gy_send=pltpu.VMEM((2, 3, HALF, D), F32),
        gy_recv=pltpu.VMEM((2, 3, HALF, D), F32),
        load_sem=dma((2,)),
        info_s=dma((7,)), info_r=dma((7,)),
        pair_s=dma((NY, 2)), pair_r=dma((NY, 2)),
        ra_s=dma((NY, 3)), ra_r=dma((NY, 3)), rb_s=dma((3,)), rb_r=dma((3,)),
        r2_s=dma((2, 3)), r2_r=dma((2, 3)),
        ex_s=dma((2, 3)), ex_r=dma((2, 3)), ey_s=dma((2, 3)), ey_r=dma((2, 3)),
        es_s=dma((2, 4)), es_r=dma((2, 4)),
        z_s=dma((2, 4, 2)), z_r=dma((2, 4, 2)),
        gp_s=dma((TILES,)), gp_r=dma((TILES,)),
        gx_s=dma((TILES, 3)), gx_r=dma((TILES, 3)), gy_s=dma((2, 3)), gy_r=dma((2, 3)),
    )
    eg, sg = pl.pallas_call(
        kernel,
        out_shape=(
            jax.ShapeDtypeStruct((Q_DEV, D), F32),
            jax.ShapeDtypeStruct((2 * BLOCK, D), F32),
        ),
        in_specs=[vmem, vmem, vmem, vmem, anyspace, anyspace],
        out_specs=(vmem, vmem),
        scratch_shapes=list(scratch.values()),
        compiler_params=pltpu.CompilerParams(
            collective_id=0, has_side_effects=True, vmem_limit_bytes=63 << 20
        ),
    )(token_ids.T, shortlist.T, positive_offsets.T, norm_gain, token_table, slab)
    return eg, sg.reshape(2 * BLOCK, 1, D)


def solution(mesh):
    return jax.shard_map(
        local,
        mesh=mesh,
        in_specs=(
            P(("dp", "label"), None),
            P("label", None),
            P(),
            P("label", None),
            P(("dp", "label"), None),
            P(("dp", "label"), None),
        ),
        out_specs=(P(("dp", "label"), None), P("dp", "label", None)),
        check_vma=False,
    )
```

```python
import math

import jax
import jax.numpy as jnp
from jax import lax
from jax.experimental import pallas as pl
from jax.experimental.pallas import tpu as pltpu
from jax.sharding import PartitionSpec as P

K = 8
POS = 2
BLOCK = 128
GCAP = 96
SEQ = 32
NX = 4
NY = 4
NZ = 8
CHIPS = NX * NY
Q_DEV = 64
Q_CHIP = 2 * Q_DEV
GROUP = CHIPS * Q_CHIP
VOC = 952
VOC_PAD = 960
LO = 192
FIELDS = 5
D = 768
BLKS = 16
SLOTS = BLKS * GCAP
HALF = Q_DEV // 2
INFO = 48
TILES = 8
TILE = 256
Q_COLS = D + 128
TOP = 32000.0
MESH = pl.DeviceIdType.MESH
F32 = jnp.float32
BF16 = jnp.bfloat16


def pack_rows(value, dst):
    largest = jnp.max(jnp.abs(value), axis=-1, keepdims=True)
    step = jnp.ceil(jnp.log(jnp.maximum(largest, 1e-30)) * (8.0 / math.log(2.0)))
    factor = jnp.exp(step * (-math.log(2.0) / 8.0)) * TOP
    dst[..., 0:D] = jnp.round(value * factor).astype(jnp.int32).astype(jnp.int16)
    dst[..., D:Q_COLS] = jnp.broadcast_to(step, value.shape[:-1] + (128,)).astype(jnp.int32).astype(jnp.int16)


def unpack_rows(src):
    step = src[..., D : D + 1].astype(jnp.int32).astype(F32)
    factor = jnp.exp(step * (math.log(2.0) / 8.0)) * (1.0 / TOP)
    return src[..., 0:D].astype(jnp.int32).astype(F32) * factor


def kernel(
    tok_hbm, list_hbm, pos_hbm, gain_hbm, table_hbm, slab_hbm,
    eg_ref, sg_ref,
    tok_ref, list_ref, pos_ref, gain_ref, table, slab, stage, row_info, info, lo_ref, w_ref, ct, tmp,
    parts, s_recv, keep, q_out, ra, rb, qa2, ra2, qb2, rb2,
    emb, rank, off2, onehot, slot_off, eacc, hgrad,
    zpart, zsend, zrecv,
    g_own, g_send, g_recv, gx_send, gx_recv, gy_send, gy_recv,
    load_sem, info_s, info_r, pair_s, pair_r, ra_s, ra_r, rb_s, rb_r, r2_s, r2_r,
    ex_s, ex_r, ey_s, ey_r, es_s, es_r, z_s, z_r,
    gp_s, gp_r, gx_s, gx_r, gy_s, gy_r,
):
    z = lax.axis_index("dp")
    label = lax.axis_index("label")
    y = lax.div(label, 2 * NX)
    x = lax.rem(lax.div(label, 2), NX)
    c = lax.rem(label, 2)
    o = 1 - c

    def lab(yy, xx, cc):
        return (yy * NX + xx) * 2 + cc

    def at_x(dx):
        return (z, lab(y, lax.rem(x + dx, NX), c))

    def at_y(dy):
        return (z, lab(lax.rem(y + dy, NY), x, c))

    sibling = (z, lab(y, x, o))
    up = (lax.rem(z + 1, NZ), label)
    down = (lax.rem(z + NZ - 1, NZ), label)

    def remote(src, dst, ssem, rsem, device):
        return pltpu.make_async_remote_copy(
            src_ref=src, dst_ref=dst, send_sem=ssem, recv_sem=rsem,
            device_id=device, device_id_type=MESH,
        )

    def send(src, dst, ssem, rsem, device):
        copy = remote(src, dst, ssem, rsem, device)
        copy.start()
        return copy

    barrier = pltpu.get_barrier_semaphore()
    row_peers = [(z, lab(y, lax.rem(x + d, NX), cc)) for d in (2, 1, 3) for cc in (c, o)]
    peers = row_peers + [sibling, up, down] + [at_y(d) for d in (1, 2, 3)]
    for device in peers:
        pl.semaphore_signal(barrier, inc=1, device_id=device, device_id_type=MESH)

    loads = [
        pltpu.make_async_copy(tok_hbm, tok_ref, load_sem.at[2]),
        pltpu.make_async_copy(list_hbm, list_ref, load_sem.at[3]),
        pltpu.make_async_copy(pos_hbm, pos_ref, load_sem.at[4]),
        pltpu.make_async_copy(gain_hbm, gain_ref, load_sem.at[5]),
    ]
    load_table = pltpu.make_async_copy(table_hbm, table.at[pl.ds(0, VOC)], load_sem.at[0])
    load_slab = pltpu.make_async_copy(slab_hbm, slab, load_sem.at[1])
    for load in loads + [load_table, load_slab]:
        load.start()

    stage[...] = jnp.zeros_like(stage)
    for load in loads:
        load.wait()
    for core in range(2):

        @pl.when(c == core)
        def _():
            for half in range(2):
                src = slice(half * HALF, (half + 1) * HALF)
                dst = slice(half * Q_DEV + core * HALF, half * Q_DEV + (core + 1) * HALF)
                stage[0:SEQ, dst] = tok_ref[:, src]
                stage[SEQ : SEQ + K, dst] = list_ref[:, src]
                stage[SEQ + K : SEQ + K + POS, dst] = pos_ref[:, src]

    row_info[0, 0] = stage[...].astype(jnp.int16)
    pl.semaphore_wait(barrier, len(peers))

    copies = []
    for d in (2, 1, 3):
        for s in range(2):
            copies.append(
                send(
                    row_info.at[0, 0], row_info.at[d, s], info_s.at[2 * d + s], info_r.at[2 * d + s],
                    (z, lab(y, lax.rem(x + d, NX), o if s else c)),
                )
            )
    copies.append(send(row_info.at[0, 0], row_info.at[0, 1], info_s.at[1], info_r.at[1], sibling))
    load_table.wait()
    table[VOC:VOC_PAD, :] = jnp.zeros((VOC_PAD - VOC, D), BF16)
    for copy in copies:
        copy.wait()
    for d in range(NX):
        both = row_info[d, 0].astype(jnp.int32) + row_info[d, 1].astype(jnp.int32)
        info[y, lax.rem(x + NX - d, NX)] = both.astype(jnp.int16)

    def info_copy(d):
        return remote(info.at[y], info.at[y], info_s.at[7 + d], info_r.at[7 + d], at_y(d))

    for d in (2, 1, 3):
        info_copy(d).start()

    base = label * VOC
    half_lo = LO // 2
    row_steps = (0, 2, 1, 3)

    def pick(index, values):
        value = values[-1]
        for n in range(len(values) - 2, -1, -1):
            value = jnp.where(index == n, values[n], value)
        return value

    order = [(0, d) for d in (2, 1, 3, 0)] + [(i, d) for i in (1, 2, 3) for d in (2, 1, 3)]
    order += [(i, 0) for i in (1, 2, 3)]
    place_of = {block: divmod(n, 2) for n, block in enumerate(order)}

    def block_of(n):
        rest = jnp.maximum(n - 4, 0)
        i = jnp.where(n < 4, 0, jnp.where(n < 13, 1 + lax.div(rest, 3), n - 12))
        third = jnp.where(n < 4, n, lax.rem(rest, 3))
        d = jnp.where(n >= 13, 0, pick(third, (2, 1, 3, 0)))
        return i, d

    def pair_copy(pair):
        return remote(parts.at[pair, :, o], s_recv.at[pair], pair_s.at[pair], pair_r.at[pair], sibling)

    def ra_copy(i, d, pair, side):
        return remote(q_out.at[pair, 2 * side], ra.at[i, d - 1], ra_s.at[i, d - 1], ra_r.at[i, d - 1], at_x(d))

    def rb_copy(i, d, step, pair, side):
        return remote(
            q_out.at[pair, 2 * side + 1], rb.at[i - 1, d], rb_s.at[i - 1, d], rb_r.at[i - 1, d], at_y(step)
        )

    def pool_pair(pair):
        for side in range(2):
            i, d = block_of(2 * pair + side)
            chip_y, chip_x = lax.rem(y + pick(i, row_steps), NY), lax.rem(x + d, NX)
            ids = info[chip_y, chip_x, 0:SEQ, :].astype(jnp.int32) - base
            valid = (ids >= 0) & (ids < VOC)
            high = (ids * 683) >> 17
            weight = jnp.ones_like(ids)
            for f in range(1, FIELDS):
                weight = jnp.where(high == f, 1 << (6 * f), weight)
            lo_ref[...] = jnp.where(valid, ids - high * LO, -1)
            w_ref[...] = jnp.where(valid, weight, 0)
            for part in range(2):
                rows = lax.broadcasted_iota(jnp.int32, (half_lo, 128), 0) + part * half_lo
                acc = jnp.zeros((half_lo, 128), jnp.int32)
                for t in range(SEQ):
                    acc = acc + jnp.where(lo_ref[t : t + 1, :] == rows, w_ref[t : t + 1, :], 0)
                for f in range(FIELDS):
                    field = (acc >> (6 * f)) & 63
                    ct[pl.ds(f * LO + part * half_lo, half_lo), pl.ds(side * 128, 128)] = (
                        field.astype(F32).astype(BF16)
                    )
        pooled = lax.dot_general(
            ct[...], table[...], (((0,), (0,)), ((), ())), preferred_element_type=F32
        )
        parts[pair] = pooled.reshape(4, 2, HALF, D)
        pair_copy(pair).start()

    def finish_pair(pair):
        pair_copy(pair).wait()
        both = parts[pair, :, c] + s_recv[pair]
        keep[pair] = both
        pack_rows(both, q_out.at[pair])
        for side in range(2):
            i, d = block_of(2 * pair + side)

            @pl.when(d != 0)
            def _():
                ra_copy(i, d, pair, side).start()

            @pl.when(i != 0)
            def _():
                rb_copy(i, d, pick(i, row_steps), pair, side).start()

    def pool_step(pair, carry):
        @pl.when(pair == 2)
        def _():
            info_copy(2).wait()

        @pl.when(pair == 3)
        def _():
            info_copy(3).wait()

        @pl.when(pair == 4)
        def _():
            info_copy(1).wait()

        pool_pair(pair)

        @pl.when(pair > 0)
        def _():
            finish_pair(pair - 1)

        return carry

    lax.fori_loop(0, TILES, pool_step, 0)

    def kept(i, d, half):
        pair, side = place_of[i, d]
        return keep[pair, 2 * side + half]

    second = []
    for d in (2, 1, 3):
        for i in (1, 2, 3):
            rb_copy(i, d, row_steps[i], *place_of[i, d]).wait()
    for d in (2, 1, 3):
        total = kept(0, d, 1)
        for i in (1, 2, 3):
            total = total + unpack_rows(rb.at[i - 1, d])
        pack_rows(total, qb2.at[d - 1])
    for d in (2, 1, 3):
        second.append(send(qb2.at[d - 1], rb2.at[d - 1], r2_s.at[1, d - 1], r2_r.at[1, d - 1], at_x(d)))
    finish_pair(TILES - 1)
    for i in (1, 2, 3):
        for d in (2, 1, 3):
            ra_copy(i, d, *place_of[i, d]).wait()
    for i in (1, 2, 3):
        total = kept(i, 0, 0)
        for d in (1, 3, 2):
            total = total + unpack_rows(ra.at[i, d - 1])
        pack_rows(total, qa2.at[i - 1])
    for i in (1, 2, 3):
        second.append(
            send(qa2.at[i - 1], ra2.at[i - 1], r2_s.at[0, i - 1], r2_r.at[0, i - 1], at_y(row_steps[i]))
        )

    before = (
        lax.broadcasted_iota(jnp.int32, (128, 128), 0) < lax.broadcasted_iota(jnp.int32, (128, 128), 1)
    ).astype(F32).astype(BF16)
    ones = jnp.ones((128, 128), BF16)
    block_ids = lax.broadcasted_iota(jnp.int32, (BLKS, 128), 0) + label * BLKS
    low_lanes = lax.broadcasted_iota(jnp.int32, (INFO - SEQ, 128), 1) < Q_DEV
    running = jnp.zeros((BLKS, 128), F32)
    for j in range(2 * TILES):
        tile, p = j // 2, j % 2
        if tile < NY:
            left = info[tile, 2 * p, SEQ:INFO, :].astype(jnp.int32)
            right = info[tile, 2 * p + 1, SEQ:INFO, :].astype(jnp.int32)
            lists = jnp.where(low_lanes, left, pltpu.roll(right, Q_DEV, 1))
        else:
            left = info[2 * p, tile - NY, SEQ:INFO, :].astype(jnp.int32)
            right = info[2 * p + 1, tile - NY, SEQ:INFO, :].astype(jnp.int32)
            lists = jnp.where(low_lanes, pltpu.roll(left, Q_DEV, 1), right)
        hit = jnp.zeros((BLKS, 128), F32)
        place = jnp.zeros((BLKS, 128), F32)
        for k in range(K):
            same = lists[k : k + 1, :] == block_ids
            hit = hit + jnp.where(same, 1.0, 0.0)
            if k < POS:
                at_row = lists[K + k : K + k + 1, :].astype(F32) + 1.0
                place = place + jnp.where(same, at_row, 0.0)
        hit16 = hit.astype(BF16)
        ahead = jnp.dot(hit16, before, preferred_element_type=F32) + running
        running = running + jnp.dot(hit16, ones, preferred_element_type=F32)
        rank[:, j, :] = jnp.where(hit > 0.0, ahead, -1.0)
        off2[:, j, :] = hit + place

    slot_ids = lax.broadcasted_iota(jnp.int32, (GCAP, 128), 0).astype(F32)

    def one_hot(b, carry):
        rows = pl.ds(pl.multiple_of(b * GCAP, GCAP), GCAP)
        found = jnp.zeros((GCAP, 128), F32)
        for j in range(2 * TILES):
            lanes = slice((j % 2) * 128, (j % 2 + 1) * 128)
            same = rank[b, j : j + 1, :] == slot_ids
            onehot[j // 2, rows, lanes] = jnp.where(same, 1.0, 0.0).astype(BF16)
            found = found + jnp.where(same, off2[b, j : j + 1, :], 0.0)
        slot_off[rows, :] = jnp.broadcast_to(jnp.sum(found, axis=1, keepdims=True), (GCAP, 128))
        return carry

    lax.fori_loop(0, BLKS // 2, one_hot, 0)

    for d in (1, 3, 2):
        ra_copy(0, d, *place_of[0, d]).wait()
    for i in (1, 2, 3):
        rb_copy(i, 0, row_steps[i], *place_of[i, 0]).wait()
    for copy in second:
        copy.wait()
    gain = gain_ref[...].reshape(1, D)
    for half in range(2):
        pooled = kept(0, 0, half)
        for n in range(3):
            pooled = pooled + unpack_rows(ra.at[0, n] if half == 0 else rb.at[n, 0])
            pooled = pooled + unpack_rows(ra2.at[n] if half == 0 else rb2.at[n])
        pooled = pooled / SEQ
        scale = lax.rsqrt(jnp.mean(pooled * pooled, axis=-1, keepdims=True) + 1e-06)
        value = (pooled * scale * gain).astype(BF16)
        if half == 0:
            emb[y, x, c] = value
        else:
            emb[NY + x, y, c] = value

    def ex_copy(half, d):
        mine = emb.at[y, x, c] if half == 0 else emb.at[NY + x, y, c]
        return remote(mine, mine, ex_s.at[half, d - 1], ex_r.at[half, d - 1], at_x(d) if half == 0 else at_y(d))

    def ey_copy(half, back, d):
        if half == 0:
            piece, device = emb.at[y, lax.rem(x + NX - back, NX), c], at_y(d)
        else:
            piece, device = emb.at[NY + x, lax.rem(y + NY - back, NY), c], at_x(d)
        return remote(piece, piece, ey_s.at[half, back, d - 1], ey_r.at[half, back, d - 1], device)

    halves = (0, 1)
    for d in (1, 3, 2):
        for half in halves:
            ex_copy(half, d).start()
    for d in (1, 3, 2):
        for half in halves:
            ey_copy(half, 0, d).start()
    lax.fori_loop(BLKS // 2, BLKS, one_hot, 0)
    for back in (1, 3, 2):
        for half in halves:
            ex_copy(half, back).wait()
            for d in (1, 3):
                ey_copy(half, back, d).start()
    for back in (1, 3, 2):
        for half in halves:
            ey_copy(half, back, 2).start()

    def forward(d):
        row = emb.at[lax.rem(y + NY - d, NY), :, c]
        col = emb.at[NY + lax.rem(x + NX - d, NX), :, c]
        return [
            send(row, row, es_s.at[0, d], es_r.at[0, d], sibling),
            send(col, col, es_s.at[1, d], es_r.at[1, d], sibling),
        ]

    pair_rows = 2 * GCAP
    chunk = SLOTS // 2

    def partial_slots(d, rows):
        tile_a = lax.rem(y + NY - d, NY)
        tile_b = NY + lax.rem(x + NX - d, NX)
        return jnp.dot(
            onehot[tile_a, rows, :], emb[tile_a].reshape(TILE, D), preferred_element_type=F32
        ) + jnp.dot(onehot[tile_b, rows, :], emb[tile_b].reshape(TILE, D), preferred_element_type=F32)

    def gather_slots(d):
        def body(m, carry):
            rows = pl.ds(pl.multiple_of(m * chunk, chunk), chunk)
            value = partial_slots(d, rows)
            eacc[rows, :] = value if d == 0 else value + eacc[rows, :]
            return carry

        lax.fori_loop(0, SLOTS // chunk, body, 0)

    def pieces_wait(d):
        for half in halves:
            for back in range(4):
                ey_copy(half, back, d).wait()

    def all_wait(copies):
        for copy in copies:
            copy.wait()

    moving = forward(0)
    all_wait(moving)
    gather_slots(0)
    pieces_wait(1)
    moving = forward(1)
    pieces_wait(3)
    moving_3 = forward(3)
    all_wait(moving)
    gather_slots(1)
    all_wait(moving_3)
    gather_slots(3)
    pieces_wait(2)
    all_wait(forward(2))
    load_slab.wait()

    row_ids = lax.broadcasted_iota(jnp.int32, (pair_rows, 2 * BLOCK), 0)
    col_ids = lax.broadcasted_iota(jnp.int32, (pair_rows, 2 * BLOCK), 1)
    same_block = (row_ids >= GCAP) == (col_ids >= BLOCK)
    col_in = jnp.where(col_ids >= BLOCK, col_ids - BLOCK, col_ids).astype(F32) + 2.0

    def grads(offset):
        dest = lax.rem(z + offset + NZ, NZ)
        srows = pl.ds(pl.multiple_of(dest * pair_rows, pair_rows), pair_rows)
        lrows = pl.ds(pl.multiple_of(dest * 2 * BLOCK, 2 * BLOCK), 2 * BLOCK)
        es_rows = (partial_slots(2, srows) + eacc[srows, :]).astype(BF16)
        labels = slab[lrows, :]
        logits = lax.dot_general(es_rows, labels, (((1,), (1,)), ((), ())), preferred_element_type=F32)
        seen = slot_off[srows, :]
        seen = jnp.concatenate([seen, seen], axis=1)
        g = jax.nn.sigmoid(logits) - jnp.where(seen == col_in, 1.0, 0.0)
        g = jnp.where(same_block & (seen > 0.0), g, 0.0).astype(BF16)
        hgrad[srows, :] = jnp.dot(g, labels, preferred_element_type=F32).astype(BF16)
        return lax.dot_general(g, es_rows, (((0,), (0,)), ((), ())), preferred_element_type=F32)

    zc = {}

    def z_send(way, step, sub):
        zc[way, step, sub] = send(
            zsend.at[way, step, sub], zrecv.at[way, step, sub],
            z_s.at[way, step, sub], z_r.at[way, step, sub], up if way == 0 else down,
        )

    def z_fill(way, step, sub, with_recv):
        value = zpart[way, step - 1, pl.ds(sub * BLOCK, BLOCK), :]
        if with_recv:
            value = value + zrecv[way, step - 1, sub].astype(F32)
        zsend[way, step, sub] = value.astype(BF16)
        z_send(way, step, sub)

    def z_pass(step, first):
        for way in range(2):
            sub = 1 - way if first else way
            zc[way, step - 1, sub].wait()
            z_fill(way, step, sub, True)

    far = grads(4)
    for way in range(2):
        zsend[way, 0, way] = far[way * BLOCK : (way + 1) * BLOCK, :].astype(BF16)
        z_send(way, 0, way)
    for way, sign in ((0, 1), (1, -1)):
        zpart[way, 0] = grads(3 * sign)
        z_fill(way, 1, 1 - way, False)
    for step in (2, 3):
        for way, sign in ((0, 1), (1, -1)):
            zpart[way, step - 1] = grads((4 - step) * sign)
    sg_ref[...] = grads(0)
    z_pass(1, False)

    def spread(tiles):
        def body(k, carry):
            grad = lax.dot_general(
                onehot[k], hgrad[...], (((0,), (0,)), ((), ())), preferred_element_type=F32
            )
            tmp[...] = grad.reshape(4, 2, HALF, D)
            for side in range(4):
                g_own[k, side] = tmp[side, c]
                g_send[k, side] = tmp[side, o].astype(BF16)
            send(g_send.at[k], g_recv.at[k], gp_s.at[k], gp_r.at[k], sibling)
            return carry

        lax.fori_loop(tiles[0], tiles[1], body, 0)

    gx = {}

    def to_chips(k):
        pltpu.make_async_remote_copy(
            src_ref=g_send.at[k], dst_ref=g_recv.at[k], send_sem=gp_s.at[k],
            recv_sem=gp_r.at[k], device_id=sibling, device_id_type=MESH,
        ).wait()
        for d in (2, 1, 3, 0):
            if k < NY:
                piece, device = lax.rem(x + d, NX), at_x(d)
            else:
                piece, device = lax.rem(y + d, NY), at_y(d)
            both = g_own[k, piece] + g_recv[k, piece].astype(F32)
            if d == 0:
                g_own[k, 0] = both
            else:
                gx_send[k, d - 1] = both.astype(BF16)
                gx[k, d] = send(
                    gx_send.at[k, d - 1], gx_recv.at[k, d - 1], gx_s.at[k, d - 1], gx_r.at[k, d - 1], device
                )

    spread((0, 2))
    spread((4, 6))
    z_pass(2, True)
    for k in (0, 4, 1, 5):
        to_chips(k)
    spread((2, 4))
    spread((6, 8))
    z_pass(2, False)
    for k in (2, 6, 3, 7):
        to_chips(k)
    z_pass(3, True)

    def own_total(k):
        total = g_own[k, 0]
        for d in (1, 3, 2):
            total = total + gx_recv[k, d - 1].astype(F32)
        return total

    for k in range(TILES):
        for d in (1, 3, 2):
            gx[k, d].wait()
    z_pass(3, False)
    copies = []
    for d in (2, 1, 3):
        gy_send[0, d - 1] = own_total(lax.rem(y + d, NY))
        copies.append(send(gy_send.at[0, d - 1], gy_recv.at[0, d - 1], gy_s.at[0, d - 1], gy_r.at[0, d - 1], at_y(d)))
        gy_send[1, d - 1] = own_total(NY + lax.rem(x + d, NX))
        copies.append(send(gy_send.at[1, d - 1], gy_recv.at[1, d - 1], gy_s.at[1, d - 1], gy_r.at[1, d - 1], at_x(d)))
    eg_ref[0:HALF, :] = own_total(y)
    eg_ref[HALF:Q_DEV, :] = own_total(NY + x)
    for copy in copies:
        copy.wait()
    for half in range(2):
        rows = pl.ds(half * HALF, HALF)
        eg_ref[rows, :] = eg_ref[rows, :] + gy_recv[half, 0] + gy_recv[half, 1] + gy_recv[half, 2]
    for first in (True, False):
        for way in range(2):
            sub = 1 - way if first else way
            zc[way, 3, sub].wait()
            rows = pl.ds(sub * BLOCK, BLOCK)
            sg_ref[rows, :] = sg_ref[rows, :] + zrecv[way, 3, sub].astype(F32)


def hand_over(eg_ref, sg_ref, eg_out, sg_out):
    eg_out[...] = eg_ref[...]
    sg_out[...] = sg_ref[...].reshape(2 * BLOCK, 1, D)


def local(token_ids, token_table, norm_gain, slab, shortlist, positive_offsets):
    vmem = pl.BlockSpec(memory_space=pltpu.VMEM)
    anyspace = pl.BlockSpec(memory_space=pl.ANY)
    dma = pltpu.SemaphoreType.DMA
    i16 = jnp.int16
    scratch = dict(
        tok_ref=pltpu.VMEM((SEQ, Q_DEV), jnp.int32),
        list_ref=pltpu.VMEM((K, Q_DEV), jnp.int32),
        pos_ref=pltpu.VMEM((POS, Q_DEV), jnp.int32),
        gain_ref=pltpu.VMEM((D,), F32),
        table=pltpu.VMEM((VOC_PAD, D), BF16),
        slab=pltpu.VMEM((BLKS * BLOCK, D), BF16),
        stage=pltpu.VMEM((INFO, 128), jnp.int32),
        row_info=pltpu.VMEM((NX, 2, INFO, 128), i16),
        info=pltpu.VMEM((NY, NX, INFO, 128), i16),
        lo_ref=pltpu.VMEM((SEQ, 128), jnp.int32),
        w_ref=pltpu.VMEM((SEQ, 128), jnp.int32),
        ct=pltpu.VMEM((VOC_PAD, 256), BF16),
        tmp=pltpu.VMEM((4, 2, HALF, D), F32),
        parts=pltpu.VMEM((TILES, 4, 2, HALF, D), F32),
        s_recv=pltpu.VMEM((TILES, 4, HALF, D), F32),
        keep=pltpu.VMEM((TILES, 4, HALF, D), F32),
        q_out=pltpu.VMEM((TILES, 4, HALF, Q_COLS), i16),
        ra=pltpu.VMEM((NY, 3, HALF, Q_COLS), i16),
        rb=pltpu.VMEM((3, NX, HALF, Q_COLS), i16),
        qa2=pltpu.VMEM((3, HALF, Q_COLS), i16),
        ra2=pltpu.VMEM((3, HALF, Q_COLS), i16),
        qb2=pltpu.VMEM((3, HALF, Q_COLS), i16),
        rb2=pltpu.VMEM((3, HALF, Q_COLS), i16),
        emb=pltpu.VMEM((TILES, 4, 2, HALF, D), BF16),
        rank=pltpu.VMEM((BLKS, 2 * TILES, 128), F32),
        off2=pltpu.VMEM((BLKS, 2 * TILES, 128), F32),
        onehot=pltpu.VMEM((TILES, SLOTS, TILE), BF16),
        slot_off=pltpu.VMEM((SLOTS, 128), F32),
        eacc=pltpu.VMEM((SLOTS, D), F32),
        hgrad=pltpu.VMEM((SLOTS, D), BF16),
        zpart=pltpu.VMEM((2, 3, 2 * BLOCK, D), F32),
        zsend=pltpu.VMEM((2, 4, 2, BLOCK, D), BF16),
        zrecv=pltpu.VMEM((2, 4, 2, BLOCK, D), BF16),
        g_own=pltpu.VMEM((TILES, 4, HALF, D), F32),
        g_send=pltpu.VMEM((TILES, 4, HALF, D), BF16),
        g_recv=pltpu.VMEM((TILES, 4, HALF, D), BF16),
        gx_send=pltpu.VMEM((TILES, 3, HALF, D), BF16),
        gx_recv=pltpu.VMEM((TILES, 3, HALF, D), BF16),
        gy_send=pltpu.VMEM((2, 3, HALF, D), F32),
        gy_recv=pltpu.VMEM((2, 3, HALF, D), F32),
        load_sem=dma((6,)),
        info_s=dma((11,)), info_r=dma((11,)),
        pair_s=dma((TILES,)), pair_r=dma((TILES,)),
        ra_s=dma((NY, 3)), ra_r=dma((NY, 3)), rb_s=dma((3, NX)), rb_r=dma((3, NX)),
        r2_s=dma((2, 3)), r2_r=dma((2, 3)),
        ex_s=dma((2, 3)), ex_r=dma((2, 3)), ey_s=dma((2, 4, 3)), ey_r=dma((2, 4, 3)),
        es_s=dma((2, 4)), es_r=dma((2, 4)),
        z_s=dma((2, 4, 2)), z_r=dma((2, 4, 2)),
        gp_s=dma((TILES,)), gp_r=dma((TILES,)),
        gx_s=dma((TILES, 3)), gx_r=dma((TILES, 3)), gy_s=dma((2, 3)), gy_r=dma((2, 3)),
    )
    eg, sg = pl.pallas_call(
        kernel,
        out_shape=(
            jax.ShapeDtypeStruct((Q_DEV, D), F32),
            jax.ShapeDtypeStruct((2 * BLOCK, D), F32),
        ),
        in_specs=[anyspace] * 6,
        out_specs=(vmem, vmem),
        scratch_shapes=list(scratch.values()),
        compiler_params=pltpu.CompilerParams(
            collective_id=0, has_side_effects=True, vmem_limit_bytes=63 << 20
        ),
    )(token_ids.T, shortlist.T, positive_offsets.T, norm_gain, token_table, slab)
    return pl.pallas_call(
        hand_over,
        out_shape=(
            jax.ShapeDtypeStruct((Q_DEV, D), F32),
            jax.ShapeDtypeStruct((2 * BLOCK, 1, D), F32),
        ),
        in_specs=[vmem, vmem],
        out_specs=(vmem, vmem),
    )(eg, sg)


def solution(mesh):
    return jax.shard_map(
        local,
        mesh=mesh,
        in_specs=(
            P(("dp", "label"), None),
            P("label", None),
            P(),
            P("label", None),
            P(("dp", "label"), None),
            P(("dp", "label"), None),
        ),
        out_specs=(P(("dp", "label"), None), P("dp", "label", None)),
        check_vma=False,
    )
```

```python
import math

import jax
import jax.numpy as jnp
from jax import lax
from jax.experimental import pallas as pl
from jax.experimental.pallas import tpu as pltpu
from jax.sharding import PartitionSpec as P

K = 8
POS = 2
BLOCK = 128
GCAP = 96
SEQ = 32
NX = 4
NY = 4
NZ = 8
CHIPS = NX * NY
Q_DEV = 64
Q_CHIP = 2 * Q_DEV
GROUP = CHIPS * Q_CHIP
VOC = 952
VOC_PAD = 960
LO = 192
FIELDS = 5
D = 768
BLKS = 16
SLOTS = BLKS * GCAP
HALF = Q_DEV // 2
INFO = 48
TILES = 8
TILE = 256
Q_COLS = D + 128
TOP = 32000.0
MESH = pl.DeviceIdType.MESH
F32 = jnp.float32
BF16 = jnp.bfloat16


def pack_rows(value, dst):
    largest = jnp.max(jnp.abs(value), axis=-1, keepdims=True)
    step = jnp.ceil(jnp.log(jnp.maximum(largest, 1e-30)) * (8.0 / math.log(2.0)))
    factor = jnp.exp(step * (-math.log(2.0) / 8.0)) * TOP
    dst[..., 0:D] = jnp.round(value * factor).astype(jnp.int32).astype(jnp.int16)
    dst[..., D:Q_COLS] = jnp.broadcast_to(step, value.shape[:-1] + (128,)).astype(jnp.int32).astype(jnp.int16)


def unpack_rows(src):
    step = src[..., D : D + 1].astype(jnp.int32).astype(F32)
    factor = jnp.exp(step * (math.log(2.0) / 8.0)) * (1.0 / TOP)
    return src[..., 0:D].astype(jnp.int32).astype(F32) * factor


def kernel(
    tok_hbm, list_hbm, pos_hbm, gain_hbm, table_hbm, slab_hbm,
    eg_ref, sg_ref,
    tok_ref, list_ref, pos_ref, gain_ref, table, slab, stage, row_info, info, lo_ref, w_ref, ct, tmp,
    parts, s_recv, keep, q_out, ra, rb, qa2, ra2, qb2, rb2,
    emb, rank, off2, onehot, slot_off, eacc, hgrad,
    zsend, zrecv,
    g_own, g_send, g_recv, gx_send, gx_recv, gy_send, gy_recv,
    load_sem, info_s, info_r, pair_s, pair_r, ra_s, ra_r, rb_s, rb_r, r2_s, r2_r,
    ex_s, ex_r, ey_s, ey_r, es_s, es_r, ef_s, ef_r, z_s, z_r,
    gp_s, gp_r, gx_s, gx_r, gy_s, gy_r,
):
    z = lax.axis_index("dp")
    label = lax.axis_index("label")
    y = lax.div(label, 2 * NX)
    x = lax.rem(lax.div(label, 2), NX)
    c = lax.rem(label, 2)
    o = 1 - c

    def lab(yy, xx, cc):
        return (yy * NX + xx) * 2 + cc

    def at_x(dx):
        return (z, lab(y, lax.rem(x + dx, NX), c))

    def at_y(dy):
        return (z, lab(lax.rem(y + dy, NY), x, c))

    sibling = (z, lab(y, x, o))
    up = (lax.rem(z + 1, NZ), label)
    down = (lax.rem(z + NZ - 1, NZ), label)

    def remote(src, dst, ssem, rsem, device):
        return pltpu.make_async_remote_copy(
            src_ref=src, dst_ref=dst, send_sem=ssem, recv_sem=rsem,
            device_id=device, device_id_type=MESH,
        )

    def send(src, dst, ssem, rsem, device):
        copy = remote(src, dst, ssem, rsem, device)
        copy.start()
        return copy

    barrier = pltpu.get_barrier_semaphore()
    row_peers = [(z, lab(y, lax.rem(x + d, NX), cc)) for d in (2, 1, 3) for cc in (c, o)]
    peers = row_peers + [sibling, up, down] + [at_y(d) for d in (1, 2, 3)]
    for device in peers:
        pl.semaphore_signal(barrier, inc=1, device_id=device, device_id_type=MESH)

    loads = [
        pltpu.make_async_copy(tok_hbm, tok_ref, load_sem.at[2]),
        pltpu.make_async_copy(list_hbm, list_ref, load_sem.at[3]),
        pltpu.make_async_copy(pos_hbm, pos_ref, load_sem.at[4]),
        pltpu.make_async_copy(gain_hbm, gain_ref, load_sem.at[5]),
    ]
    load_table = pltpu.make_async_copy(table_hbm, table.at[pl.ds(0, VOC)], load_sem.at[0])
    load_slab = pltpu.make_async_copy(slab_hbm, slab, load_sem.at[1])
    for load in loads + [load_table, load_slab]:
        load.start()

    stage[...] = jnp.zeros_like(stage)
    for load in loads:
        load.wait()
    for core in range(2):

        @pl.when(c == core)
        def _():
            for half in range(2):
                src = slice(half * HALF, (half + 1) * HALF)
                dst = slice(half * Q_DEV + core * HALF, half * Q_DEV + (core + 1) * HALF)
                stage[0:SEQ, dst] = tok_ref[:, src]
                stage[SEQ : SEQ + K, dst] = list_ref[:, src]
                stage[SEQ + K : SEQ + K + POS, dst] = pos_ref[:, src]

    row_info[0, 0] = stage[...].astype(jnp.int16)
    pl.semaphore_wait(barrier, len(peers))

    copies = []
    for d in (2, 1, 3):
        for s in range(2):
            copies.append(
                send(
                    row_info.at[0, 0], row_info.at[d, s], info_s.at[2 * d + s], info_r.at[2 * d + s],
                    (z, lab(y, lax.rem(x + d, NX), o if s else c)),
                )
            )
    copies.append(send(row_info.at[0, 0], row_info.at[0, 1], info_s.at[1], info_r.at[1], sibling))
    load_table.wait()
    table[VOC:VOC_PAD, :] = jnp.zeros((VOC_PAD - VOC, D), BF16)
    for copy in copies:
        copy.wait()
    for d in range(NX):
        both = row_info[d, 0].astype(jnp.int32) + row_info[d, 1].astype(jnp.int32)
        info[y, lax.rem(x + NX - d, NX)] = both.astype(jnp.int16)

    def info_copy(d):
        return remote(info.at[y], info.at[y], info_s.at[7 + d], info_r.at[7 + d], at_y(d))

    for d in (2, 1, 3):
        info_copy(d).start()

    base = label * VOC
    half_lo = LO // 2
    row_steps = (0, 2, 1, 3)

    def pick(index, values):
        value = values[-1]
        for n in range(len(values) - 2, -1, -1):
            value = jnp.where(index == n, values[n], value)
        return value

    order = [(0, d) for d in (2, 1, 3, 0)] + [(i, d) for i in (1, 2, 3) for d in (2, 1, 3)]
    order += [(i, 0) for i in (1, 2, 3)]
    place_of = {block: divmod(n, 2) for n, block in enumerate(order)}

    def block_of(n):
        rest = jnp.maximum(n - 4, 0)
        i = jnp.where(n < 4, 0, jnp.where(n < 13, 1 + lax.div(rest, 3), n - 12))
        third = jnp.where(n < 4, n, lax.rem(rest, 3))
        d = jnp.where(n >= 13, 0, pick(third, (2, 1, 3, 0)))
        return i, d

    def pair_copy(pair):
        return remote(parts.at[pair, :, o], s_recv.at[pair], pair_s.at[pair], pair_r.at[pair], sibling)

    def ra_copy(i, d, pair, side):
        return remote(q_out.at[pair, 2 * side], ra.at[i, d - 1], ra_s.at[i, d - 1], ra_r.at[i, d - 1], at_x(d))

    def rb_copy(i, d, step, pair, side):
        return remote(
            q_out.at[pair, 2 * side + 1], rb.at[i - 1, d], rb_s.at[i - 1, d], rb_r.at[i - 1, d], at_y(step)
        )

    def pool_pair(pair):
        for side in range(2):
            i, d = block_of(2 * pair + side)
            chip_y, chip_x = lax.rem(y + pick(i, row_steps), NY), lax.rem(x + d, NX)
            ids = info[chip_y, chip_x, 0:SEQ, :].astype(jnp.int32) - base
            valid = (ids >= 0) & (ids < VOC)
            high = (ids * 683) >> 17
            weight = jnp.ones_like(ids)
            for f in range(1, FIELDS):
                weight = jnp.where(high == f, 1 << (6 * f), weight)
            lo_ref[...] = jnp.where(valid, ids - high * LO, -1)
            w_ref[...] = jnp.where(valid, weight, 0)
            for part in range(2):
                rows = lax.broadcasted_iota(jnp.int32, (half_lo, 128), 0) + part * half_lo
                acc = jnp.zeros((half_lo, 128), jnp.int32)
                for t in range(SEQ):
                    acc = acc + jnp.where(lo_ref[t : t + 1, :] == rows, w_ref[t : t + 1, :], 0)
                for f in range(FIELDS):
                    field = (acc >> (6 * f)) & 63
                    ct[pl.ds(f * LO + part * half_lo, half_lo), pl.ds(side * 128, 128)] = (
                        field.astype(F32).astype(BF16)
                    )
        pooled = lax.dot_general(
            ct[...], table[...], (((0,), (0,)), ((), ())), preferred_element_type=F32
        )
        parts[pair] = pooled.reshape(4, 2, HALF, D)
        pair_copy(pair).start()

    def finish_pair(pair):
        pair_copy(pair).wait()
        both = parts[pair, :, c] + s_recv[pair]
        keep[pair] = both
        pack_rows(both, q_out.at[pair])
        for side in range(2):
            i, d = block_of(2 * pair + side)

            @pl.when(d != 0)
            def _():
                ra_copy(i, d, pair, side).start()

            @pl.when(i != 0)
            def _():
                rb_copy(i, d, pick(i, row_steps), pair, side).start()

    def pool_step(pair, carry):
        @pl.when(pair == 2)
        def _():
            info_copy(2).wait()

        @pl.when(pair == 3)
        def _():
            info_copy(3).wait()

        @pl.when(pair == 4)
        def _():
            info_copy(1).wait()

        pool_pair(pair)

        @pl.when(pair > 0)
        def _():
            finish_pair(pair - 1)

        return carry

    lax.fori_loop(0, TILES, pool_step, 0)

    def kept(i, d, half):
        pair, side = place_of[i, d]
        return keep[pair, 2 * side + half]

    second = []
    for d in (2, 1, 3):
        for i in (1, 2, 3):
            rb_copy(i, d, row_steps[i], *place_of[i, d]).wait()
    for d in (2, 1, 3):
        total = kept(0, d, 1)
        for i in (1, 2, 3):
            total = total + unpack_rows(rb.at[i - 1, d])
        pack_rows(total, qb2.at[d - 1])
    for d in (2, 1, 3):
        second.append(send(qb2.at[d - 1], rb2.at[d - 1], r2_s.at[1, d - 1], r2_r.at[1, d - 1], at_x(d)))
    for i in (1, 2, 3):
        for d in (2, 1, 3):
            ra_copy(i, d, *place_of[i, d]).wait()
    from_x = [sum(unpack_rows(ra.at[i, d]) for d in range(3)) for i in (1, 2, 3)]
    finish_pair(TILES - 1)
    for i in (1, 2, 3):
        pack_rows(kept(i, 0, 0) + from_x[i - 1], qa2.at[i - 1])
    for i in (1, 2, 3):
        second.append(
            send(qa2.at[i - 1], ra2.at[i - 1], r2_s.at[0, i - 1], r2_r.at[0, i - 1], at_y(row_steps[i]))
        )

    before = (
        lax.broadcasted_iota(jnp.int32, (128, 128), 0) < lax.broadcasted_iota(jnp.int32, (128, 128), 1)
    ).astype(F32).astype(BF16)
    ones = jnp.ones((128, 128), BF16)
    block_ids = lax.broadcasted_iota(jnp.int32, (BLKS, 128), 0) + label * BLKS
    low_lanes = lax.broadcasted_iota(jnp.int32, (INFO - SEQ, 128), 1) < Q_DEV
    running = jnp.zeros((BLKS, 128), F32)
    for j in range(2 * TILES):
        tile, p = j // 2, j % 2
        if tile < NY:
            left = info[tile, 2 * p, SEQ:INFO, :].astype(jnp.int32)
            right = info[tile, 2 * p + 1, SEQ:INFO, :].astype(jnp.int32)
            lists = jnp.where(low_lanes, left, pltpu.roll(right, Q_DEV, 1))
        else:
            left = info[2 * p, tile - NY, SEQ:INFO, :].astype(jnp.int32)
            right = info[2 * p + 1, tile - NY, SEQ:INFO, :].astype(jnp.int32)
            lists = jnp.where(low_lanes, pltpu.roll(left, Q_DEV, 1), right)
        hit = jnp.zeros((BLKS, 128), F32)
        place = jnp.zeros((BLKS, 128), F32)
        for k in range(K):
            same = lists[k : k + 1, :] == block_ids
            hit = hit + jnp.where(same, 1.0, 0.0)
            if k < POS:
                at_row = lists[K + k : K + k + 1, :].astype(F32) + 1.0
                place = place + jnp.where(same, at_row, 0.0)
        hit16 = hit.astype(BF16)
        ahead = jnp.dot(hit16, before, preferred_element_type=F32) + running
        running = running + jnp.dot(hit16, ones, preferred_element_type=F32)
        rank[:, j, :] = jnp.where(hit > 0.0, ahead, -1.0)
        off2[:, j, :] = hit + place

    slot_ids = lax.broadcasted_iota(jnp.int32, (GCAP, 128), 0).astype(F32)

    def one_hot(b, carry):
        rows = pl.ds(pl.multiple_of(b * GCAP, GCAP), GCAP)
        found = jnp.zeros((GCAP, 128), F32)
        for j in range(2 * TILES):
            lanes = slice((j % 2) * 128, (j % 2 + 1) * 128)
            same = rank[b, j : j + 1, :] == slot_ids
            onehot[j // 2, rows, lanes] = jnp.where(same, 1.0, 0.0).astype(BF16)
            found = found + jnp.where(same, off2[b, j : j + 1, :], 0.0)
        slot_off[rows, :] = jnp.broadcast_to(jnp.sum(found, axis=1, keepdims=True), (GCAP, 128))
        return carry

    lax.fori_loop(0, BLKS // 2, one_hot, 0)

    for d in (1, 3, 2):
        ra_copy(0, d, *place_of[0, d]).wait()
    for copy in second[0:3]:
        copy.wait()
    near = [
        kept(0, 0, 0) + sum(unpack_rows(ra.at[0, n]) for n in range(3)),
        kept(0, 0, 1) + sum(unpack_rows(rb2.at[n]) for n in range(3)),
    ]
    for i in (1, 2, 3):
        rb_copy(i, 0, row_steps[i], *place_of[i, 0]).wait()
    for copy in second[3:6]:
        copy.wait()
    gain = gain_ref[...].reshape(1, D)
    for half in range(2):
        pooled = near[half]
        for n in range(3):
            pooled = pooled + unpack_rows(ra2.at[n] if half == 0 else rb.at[n, 0])
        pooled = pooled / SEQ
        scale = lax.rsqrt(jnp.mean(pooled * pooled, axis=-1, keepdims=True) + 1e-06)
        value = (pooled * scale * gain).astype(BF16)
        if half == 0:
            emb[y, x, c] = value
        else:
            emb[NY + x, y, c] = value

    def ex_copy(half, d):
        mine = emb.at[y, x, c] if half == 0 else emb.at[NY + x, y, c]
        return remote(mine, mine, ex_s.at[half, d - 1], ex_r.at[half, d - 1], at_x(d) if half == 0 else at_y(d))

    def ey_copy(half, back, d):
        if half == 0:
            piece, device = emb.at[y, lax.rem(x + NX - back, NX), c], at_y(d)
        else:
            piece, device = emb.at[NY + x, lax.rem(y + NY - back, NY), c], at_x(d)
        return remote(piece, piece, ey_s.at[half, back, d - 1], ey_r.at[half, back, d - 1], device)

    halves = (0, 1)
    for d in (1, 3, 2):
        for half in halves:
            ex_copy(half, d).start()
    lax.fori_loop(BLKS // 2, BLKS, one_hot, 0)
    for d in (1, 3, 2):
        for half in halves:
            ey_copy(half, 0, d).start()
    for back in (1, 3, 2):
        for half in halves:
            ex_copy(half, back).wait()
            for d in (1, 3):
                ey_copy(half, back, d).start()
    for back in (1, 3, 2):
        for half in halves:
            ey_copy(half, back, 2).start()

    def forward(d):
        row = emb.at[lax.rem(y + NY - d, NY), :, c]
        col = emb.at[NY + lax.rem(x + NX - d, NX), :, c]
        return [
            send(row, row, es_s.at[0, d], es_r.at[0, d], sibling),
            send(col, col, es_s.at[1, d], es_r.at[1, d], sibling),
        ]

    pair_rows = 2 * GCAP
    chunk = SLOTS // 2

    def partial_slots(d, rows):
        tile_a = lax.rem(y + NY - d, NY)
        tile_b = NY + lax.rem(x + NX - d, NX)
        return jnp.dot(
            onehot[tile_a, rows, :], emb[tile_a].reshape(TILE, D), preferred_element_type=F32
        ) + jnp.dot(onehot[tile_b, rows, :], emb[tile_b].reshape(TILE, D), preferred_element_type=F32)

    def gather_slots(d):
        def body(m, carry):
            rows = pl.ds(pl.multiple_of(m * chunk, chunk), chunk)
            value = partial_slots(d, rows)
            eacc[rows, :] = value if d == 0 else value + eacc[rows, :]
            return carry

        lax.fori_loop(0, SLOTS // chunk, body, 0)

    def pieces_wait(d):
        for half in halves:
            for back in range(4):
                ey_copy(half, back, d).wait()

    def all_wait(copies):
        for copy in copies:
            copy.wait()

    moving = forward(0)
    all_wait(moving)
    gather_slots(0)
    pieces_wait(1)
    moving = forward(1)
    pieces_wait(3)
    moving_3 = forward(3)
    all_wait(moving)
    gather_slots(1)
    all_wait(moving_3)
    moving = []
    for back in (0, 1, 3, 2):
        for half in halves:
            ey_copy(half, back, 2).wait()
            if half == 0:
                piece = emb.at[lax.rem(y + 2, NY), lax.rem(x + NX - back, NX), c]
            else:
                piece = emb.at[NY + lax.rem(x + 2, NX), lax.rem(y + NY - back, NY), c]
            moving.append(send(piece, piece, ef_s.at[half, back], ef_r.at[half, back], sibling))
    gather_slots(3)
    all_wait(moving)
    load_slab.wait()

    row_ids = lax.broadcasted_iota(jnp.int32, (pair_rows, 2 * BLOCK), 0)
    col_ids = lax.broadcasted_iota(jnp.int32, (pair_rows, 2 * BLOCK), 1)
    same_block = (row_ids >= GCAP) == (col_ids >= BLOCK)
    col_in = jnp.where(col_ids >= BLOCK, col_ids - BLOCK, col_ids).astype(F32) + 2.0

    def grads(offset):
        dest = lax.rem(z + offset + NZ, NZ)
        srows = pl.ds(pl.multiple_of(dest * pair_rows, pair_rows), pair_rows)
        lrows = pl.ds(pl.multiple_of(dest * 2 * BLOCK, 2 * BLOCK), 2 * BLOCK)
        es_rows = (partial_slots(2, srows) + eacc[srows, :]).astype(BF16)
        labels = slab[lrows, :]
        logits = lax.dot_general(es_rows, labels, (((1,), (1,)), ((), ())), preferred_element_type=F32)
        seen = slot_off[srows, :]
        seen = jnp.concatenate([seen, seen], axis=1)
        g = jax.nn.sigmoid(logits) - jnp.where(seen == col_in, 1.0, 0.0)
        g = jnp.where(same_block & (seen > 0.0), g, 0.0).astype(BF16)
        hgrad[srows, :] = jnp.dot(g, labels, preferred_element_type=F32).astype(BF16)
        return lax.dot_general(g, es_rows, (((0,), (0,)), ((), ())), preferred_element_type=F32)

    zc = {}

    def z_send(way, step, sub):
        zc[way, step, sub] = send(
            zsend.at[way, step, sub], zrecv.at[way, step, sub],
            z_s.at[way, step, sub], z_r.at[way, step, sub], up if way == 0 else down,
        )

    def z_fill(way, step, sub, with_recv):
        value = parts[3 * way + step - 1, pl.ds(2 * sub, 2)].reshape(BLOCK, D)
        if with_recv:
            value = value + zrecv[way, step - 1, sub].astype(F32)
        zsend[way, step, sub] = value.astype(BF16)
        z_send(way, step, sub)

    def z_pass(step, first):
        for way in range(2):
            sub = 1 - way if first else way
            zc[way, step - 1, sub].wait()
            z_fill(way, step, sub, True)

    far = grads(4)
    for way in range(2):
        zsend[way, 0, way] = far[way * BLOCK : (way + 1) * BLOCK, :].astype(BF16)
        z_send(way, 0, way)
    for way, sign in ((0, 1), (1, -1)):
        parts[3 * way] = grads(3 * sign).reshape(4, 2, HALF, D)
        z_fill(way, 1, 1 - way, False)
    for step in (2, 3):
        for way, sign in ((0, 1), (1, -1)):
            parts[3 * way + step - 1] = grads((4 - step) * sign).reshape(4, 2, HALF, D)
    sg_ref[...] = grads(0)
    z_pass(1, False)

    def spread(tiles):
        def body(k, carry):
            grad = lax.dot_general(
                onehot[k], hgrad[...], (((0,), (0,)), ((), ())), preferred_element_type=F32
            )
            tmp[...] = grad.reshape(4, 2, HALF, D)
            for side in range(4):
                g_own[k, side] = tmp[side, c]
                g_send[k, side] = tmp[side, o].astype(BF16)
            send(g_send.at[k], g_recv.at[k], gp_s.at[k], gp_r.at[k], sibling)
            return carry

        lax.fori_loop(tiles[0], tiles[1], body, 0)

    gx = {}

    def to_chips(k):
        pltpu.make_async_remote_copy(
            src_ref=g_send.at[k], dst_ref=g_recv.at[k], send_sem=gp_s.at[k],
            recv_sem=gp_r.at[k], device_id=sibling, device_id_type=MESH,
        ).wait()
        for d in (2, 1, 3, 0):
            if k < NY:
                piece, device = lax.rem(x + d, NX), at_x(d)
            else:
                piece, device = lax.rem(y + d, NY), at_y(d)
            both = g_own[k, piece] + g_recv[k, piece].astype(F32)
            if d == 0:
                g_own[k, 0] = both
            else:
                gx_send[k, d - 1] = both.astype(BF16)
                gx[k, d] = send(
                    gx_send.at[k, d - 1], gx_recv.at[k, d - 1], gx_s.at[k, d - 1], gx_r.at[k, d - 1], device
                )

    spread((0, 2))
    spread((4, 6))
    z_pass(2, True)
    for k in (0, 4, 1, 5):
        to_chips(k)
    spread((2, 4))
    spread((6, 8))
    z_pass(2, False)
    for k in (2, 6, 3, 7):
        to_chips(k)
    z_pass(3, True)

    def own_total(k):
        total = g_own[k, 0]
        for d in (1, 3, 2):
            total = total + gx_recv[k, d - 1].astype(F32)
        return total

    for k in range(TILES):
        for d in (1, 3, 2):
            gx[k, d].wait()
    z_pass(3, False)
    copies = []
    for d in (2, 1, 3):
        pack_rows(own_total(lax.rem(y + d, NY)), gy_send.at[0, d - 1])
        copies.append(send(gy_send.at[0, d - 1], gy_recv.at[0, d - 1], gy_s.at[0, d - 1], gy_r.at[0, d - 1], at_y(d)))
        pack_rows(own_total(NY + lax.rem(x + d, NX)), gy_send.at[1, d - 1])
        copies.append(send(gy_send.at[1, d - 1], gy_recv.at[1, d - 1], gy_s.at[1, d - 1], gy_r.at[1, d - 1], at_x(d)))
    eg_ref[0:HALF, :] = own_total(y)
    eg_ref[HALF:Q_DEV, :] = own_total(NY + x)
    for copy in copies:
        copy.wait()
    for half in range(2):
        rows = pl.ds(half * HALF, HALF)
        eg_ref[rows, :] = eg_ref[rows, :] + sum(unpack_rows(gy_recv.at[half, n]) for n in range(3))
    for first in (True, False):
        for way in range(2):
            sub = 1 - way if first else way
            zc[way, 3, sub].wait()
            rows = pl.ds(sub * BLOCK, BLOCK)
            sg_ref[rows, :] = sg_ref[rows, :] + zrecv[way, 3, sub].astype(F32)


def hand_over(eg_ref, sg_ref, eg_out, sg_out):
    eg_out[...] = eg_ref[...]
    sg_out[...] = sg_ref[...].reshape(2 * BLOCK, 1, D)


def local(token_ids, token_table, norm_gain, slab, shortlist, positive_offsets):
    vmem = pl.BlockSpec(memory_space=pltpu.VMEM)
    anyspace = pl.BlockSpec(memory_space=pl.ANY)
    dma = pltpu.SemaphoreType.DMA
    i16 = jnp.int16
    scratch = dict(
        tok_ref=pltpu.VMEM((SEQ, Q_DEV), jnp.int32),
        list_ref=pltpu.VMEM((K, Q_DEV), jnp.int32),
        pos_ref=pltpu.VMEM((POS, Q_DEV), jnp.int32),
        gain_ref=pltpu.VMEM((D,), F32),
        table=pltpu.VMEM((VOC_PAD, D), BF16),
        slab=pltpu.VMEM((BLKS * BLOCK, D), BF16),
        stage=pltpu.VMEM((INFO, 128), jnp.int32),
        row_info=pltpu.VMEM((NX, 2, INFO, 128), i16),
        info=pltpu.VMEM((NY, NX, INFO, 128), i16),
        lo_ref=pltpu.VMEM((SEQ, 128), jnp.int32),
        w_ref=pltpu.VMEM((SEQ, 128), jnp.int32),
        ct=pltpu.VMEM((VOC_PAD, 256), BF16),
        tmp=pltpu.VMEM((4, 2, HALF, D), F32),
        parts=pltpu.VMEM((TILES, 4, 2, HALF, D), F32),
        s_recv=pltpu.VMEM((TILES, 4, HALF, D), F32),
        keep=pltpu.VMEM((TILES, 4, HALF, D), F32),
        q_out=pltpu.VMEM((TILES, 4, HALF, Q_COLS), i16),
        ra=pltpu.VMEM((NY, 3, HALF, Q_COLS), i16),
        rb=pltpu.VMEM((3, NX, HALF, Q_COLS), i16),
        qa2=pltpu.VMEM((3, HALF, Q_COLS), i16),
        ra2=pltpu.VMEM((3, HALF, Q_COLS), i16),
        qb2=pltpu.VMEM((3, HALF, Q_COLS), i16),
        rb2=pltpu.VMEM((3, HALF, Q_COLS), i16),
        emb=pltpu.VMEM((TILES, 4, 2, HALF, D), BF16),
        rank=pltpu.VMEM((BLKS, 2 * TILES, 128), F32),
        off2=pltpu.VMEM((BLKS, 2 * TILES, 128), F32),
        onehot=pltpu.VMEM((TILES, SLOTS, TILE), BF16),
        slot_off=pltpu.VMEM((SLOTS, 128), F32),
        eacc=pltpu.VMEM((SLOTS, D), F32),
        hgrad=pltpu.VMEM((SLOTS, D), BF16),
        zsend=pltpu.VMEM((2, 4, 2, BLOCK, D), BF16),
        zrecv=pltpu.VMEM((2, 4, 2, BLOCK, D), BF16),
        g_own=pltpu.VMEM((TILES, 4, HALF, D), F32),
        g_send=pltpu.VMEM((TILES, 4, HALF, D), BF16),
        g_recv=pltpu.VMEM((TILES, 4, HALF, D), BF16),
        gx_send=pltpu.VMEM((TILES, 3, HALF, D), BF16),
        gx_recv=pltpu.VMEM((TILES, 3, HALF, D), BF16),
        gy_send=pltpu.VMEM((2, 3, HALF, Q_COLS), i16),
        gy_recv=pltpu.VMEM((2, 3, HALF, Q_COLS), i16),
        load_sem=dma((6,)),
        info_s=dma((11,)), info_r=dma((11,)),
        pair_s=dma((TILES,)), pair_r=dma((TILES,)),
        ra_s=dma((NY, 3)), ra_r=dma((NY, 3)), rb_s=dma((3, NX)), rb_r=dma((3, NX)),
        r2_s=dma((2, 3)), r2_r=dma((2, 3)),
        ex_s=dma((2, 3)), ex_r=dma((2, 3)), ey_s=dma((2, 4, 3)), ey_r=dma((2, 4, 3)),
        es_s=dma((2, 4)), es_r=dma((2, 4)), ef_s=dma((2, 4)), ef_r=dma((2, 4)),
        z_s=dma((2, 4, 2)), z_r=dma((2, 4, 2)),
        gp_s=dma((TILES,)), gp_r=dma((TILES,)),
        gx_s=dma((TILES, 3)), gx_r=dma((TILES, 3)), gy_s=dma((2, 3)), gy_r=dma((2, 3)),
    )
    eg, sg = pl.pallas_call(
        kernel,
        out_shape=(
            jax.ShapeDtypeStruct((Q_DEV, D), F32),
            jax.ShapeDtypeStruct((2 * BLOCK, D), F32),
        ),
        in_specs=[anyspace] * 6,
        out_specs=(vmem, vmem),
        scratch_shapes=list(scratch.values()),
        compiler_params=pltpu.CompilerParams(
            collective_id=0, has_side_effects=True, vmem_limit_bytes=57 << 20
        ),
    )(token_ids.T, shortlist.T, positive_offsets.T, norm_gain, token_table, slab)
    return pl.pallas_call(
        hand_over,
        out_shape=(
            jax.ShapeDtypeStruct((Q_DEV, D), F32),
            jax.ShapeDtypeStruct((2 * BLOCK, 1, D), F32),
        ),
        in_specs=[vmem, vmem],
        out_specs=(vmem, vmem),
    )(eg, sg)


def solution(mesh):
    return jax.shard_map(
        local,
        mesh=mesh,
        in_specs=(
            P(("dp", "label"), None),
            P("label", None),
            P(),
            P("label", None),
            P(("dp", "label"), None),
            P(("dp", "label"), None),
        ),
        out_specs=(P(("dp", "label"), None), P("dp", "label", None)),
        check_vma=False,
    )
```

```python
import math

import jax
import jax.numpy as jnp
from jax import lax
from jax.experimental import pallas as pl
from jax.experimental.pallas import tpu as pltpu
from jax.sharding import PartitionSpec as P

K = 8
POS = 2
BLOCK = 128
GCAP = 96
SEQ = 32
NX = 4
NY = 4
NZ = 8
CHIPS = NX * NY
Q_DEV = 64
Q_CHIP = 2 * Q_DEV
GROUP = CHIPS * Q_CHIP
VOC = 952
VOC_PAD = 960
LO = 192
FIELDS = 5
D = 768
BLKS = 16
SLOTS = BLKS * GCAP
HALF = Q_DEV // 2
INFO = 48
TILES = 8
TILE = 256
Q_COLS = D + 128
TOP = 32000.0
MESH = pl.DeviceIdType.MESH
F32 = jnp.float32
BF16 = jnp.bfloat16


def pack_rows(value, dst):
    largest = jnp.max(jnp.abs(value), axis=-1, keepdims=True)
    step = jnp.ceil(jnp.log(jnp.maximum(largest, 1e-30)) * (8.0 / math.log(2.0)))
    factor = jnp.exp(step * (-math.log(2.0) / 8.0)) * TOP
    dst[..., 0:D] = jnp.round(value * factor).astype(jnp.int32).astype(jnp.int16)
    dst[..., D:Q_COLS] = jnp.broadcast_to(step, value.shape[:-1] + (128,)).astype(jnp.int32).astype(jnp.int16)


def unpack_rows(src):
    step = src[..., D : D + 1].astype(jnp.int32).astype(F32)
    factor = jnp.exp(step * (math.log(2.0) / 8.0)) * (1.0 / TOP)
    return src[..., 0:D].astype(jnp.int32).astype(F32) * factor


def kernel(
    tok_hbm, list_hbm, pos_hbm, gain_hbm, table_hbm, slab_hbm,
    eg_ref, sg_ref,
    tok_ref, list_ref, pos_ref, gain_ref, table, slab, stage, row_info, info, lo_ref, w_ref, ct, tmp,
    parts, s_recv, keep, q_out, ra, rb, qa2, ra2, qb2, rb2,
    emb, rank, off2, onehot, slot_off, eacc, hgrad,
    zsend, zrecv,
    g_own, g_send, g_recv, gx_send, gx_recv, gy_send, gy_recv,
    load_sem, info_s, info_r, pair_s, pair_r, ra_s, ra_r, rb_s, rb_r, r2_s, r2_r,
    ex_s, ex_r, ey_s, ey_r, es_s, es_r, er_s, er_r, ef_s, ef_r, z_s, z_r,
    gp_s, gp_r, gx_s, gx_r, gy_s, gy_r,
):
    z = lax.axis_index("dp")
    label = lax.axis_index("label")
    y = lax.div(label, 2 * NX)
    x = lax.rem(lax.div(label, 2), NX)
    c = lax.rem(label, 2)
    o = 1 - c

    def lab(yy, xx, cc):
        return (yy * NX + xx) * 2 + cc

    def at_x(dx):
        return (z, lab(y, lax.rem(x + dx, NX), c))

    def at_y(dy):
        return (z, lab(lax.rem(y + dy, NY), x, c))

    sibling = (z, lab(y, x, o))
    up = (lax.rem(z + 1, NZ), label)
    down = (lax.rem(z + NZ - 1, NZ), label)

    def remote(src, dst, ssem, rsem, device):
        return pltpu.make_async_remote_copy(
            src_ref=src, dst_ref=dst, send_sem=ssem, recv_sem=rsem,
            device_id=device, device_id_type=MESH,
        )

    def send(src, dst, ssem, rsem, device):
        copy = remote(src, dst, ssem, rsem, device)
        copy.start()
        return copy

    barrier = pltpu.get_barrier_semaphore()
    row_peers = [(z, lab(y, lax.rem(x + d, NX), cc)) for d in (2, 1, 3) for cc in (c, o)]
    peers = row_peers + [sibling, up, down] + [at_y(d) for d in (1, 2, 3)]
    for device in peers:
        pl.semaphore_signal(barrier, inc=1, device_id=device, device_id_type=MESH)

    loads = [
        pltpu.make_async_copy(tok_hbm, tok_ref, load_sem.at[2]),
        pltpu.make_async_copy(list_hbm, list_ref, load_sem.at[3]),
        pltpu.make_async_copy(pos_hbm, pos_ref, load_sem.at[4]),
        pltpu.make_async_copy(gain_hbm, gain_ref, load_sem.at[5]),
    ]
    load_table = pltpu.make_async_copy(table_hbm, table.at[pl.ds(0, VOC)], load_sem.at[0])
    load_slab = pltpu.make_async_copy(slab_hbm, slab, load_sem.at[1])
    for load in loads + [load_table, load_slab]:
        load.start()

    stage[...] = jnp.zeros_like(stage)
    for load in loads:
        load.wait()
    for core in range(2):

        @pl.when(c == core)
        def _():
            for half in range(2):
                src = slice(half * HALF, (half + 1) * HALF)
                dst = slice(half * Q_DEV + core * HALF, half * Q_DEV + (core + 1) * HALF)
                stage[0:SEQ, dst] = tok_ref[:, src]
                stage[SEQ : SEQ + K, dst] = list_ref[:, src]
                stage[SEQ + K : SEQ + K + POS, dst] = pos_ref[:, src]

    row_info[0, 0] = stage[...].astype(jnp.int16)
    pl.semaphore_wait(barrier, len(peers))

    copies = []
    for d in (2, 1, 3):
        for s in range(2):
            copies.append(
                send(
                    row_info.at[0, 0], row_info.at[d, s], info_s.at[2 * d + s], info_r.at[2 * d + s],
                    (z, lab(y, lax.rem(x + d, NX), o if s else c)),
                )
            )
    copies.append(send(row_info.at[0, 0], row_info.at[0, 1], info_s.at[1], info_r.at[1], sibling))
    load_table.wait()
    table[VOC:VOC_PAD, :] = jnp.zeros((VOC_PAD - VOC, D), BF16)
    for copy in copies:
        copy.wait()
    for d in range(NX):
        both = row_info[d, 0].astype(jnp.int32) + row_info[d, 1].astype(jnp.int32)
        info[y, lax.rem(x + NX - d, NX)] = both.astype(jnp.int16)

    def info_copy(d):
        return remote(info.at[y], info.at[y], info_s.at[7 + d], info_r.at[7 + d], at_y(d))

    for d in (2, 1, 3):
        info_copy(d).start()

    base = label * VOC
    half_lo = LO // 2
    row_steps = (0, 2, 1, 3)

    def pick(index, values):
        value = values[-1]
        for n in range(len(values) - 2, -1, -1):
            value = jnp.where(index == n, values[n], value)
        return value

    order = [(0, d) for d in (2, 1, 3, 0)] + [(i, d) for i in (1, 2, 3) for d in (2, 1, 3)]
    order += [(i, 0) for i in (1, 2, 3)]
    place_of = {block: divmod(n, 2) for n, block in enumerate(order)}

    def block_of(n):
        rest = jnp.maximum(n - 4, 0)
        i = jnp.where(n < 4, 0, jnp.where(n < 13, 1 + lax.div(rest, 3), n - 12))
        third = jnp.where(n < 4, n, lax.rem(rest, 3))
        d = jnp.where(n >= 13, 0, pick(third, (2, 1, 3, 0)))
        return i, d

    def pair_copy(pair):
        return remote(parts.at[pair, :, o], s_recv.at[pair], pair_s.at[pair], pair_r.at[pair], sibling)

    def ra_copy(i, d, pair, side):
        return remote(q_out.at[pair, 2 * side], ra.at[i, d - 1], ra_s.at[i, d - 1], ra_r.at[i, d - 1], at_x(d))

    def rb_copy(i, d, step, pair, side):
        return remote(
            q_out.at[pair, 2 * side + 1], rb.at[i - 1, d], rb_s.at[i - 1, d], rb_r.at[i - 1, d], at_y(step)
        )

    def pool_pair(pair):
        for side in range(2):
            i, d = block_of(2 * pair + side)
            chip_y, chip_x = lax.rem(y + pick(i, row_steps), NY), lax.rem(x + d, NX)
            ids = info[chip_y, chip_x, 0:SEQ, :].astype(jnp.int32) - base
            valid = (ids >= 0) & (ids < VOC)
            high = (ids * 683) >> 17
            weight = jnp.ones_like(ids)
            for f in range(1, FIELDS):
                weight = jnp.where(high == f, 1 << (6 * f), weight)
            lo_ref[...] = jnp.where(valid, ids - high * LO, -1)
            w_ref[...] = jnp.where(valid, weight, 0)
            for part in range(2):
                rows = lax.broadcasted_iota(jnp.int32, (half_lo, 128), 0) + part * half_lo
                acc = jnp.zeros((half_lo, 128), jnp.int32)
                for t in range(SEQ):
                    acc = acc + jnp.where(lo_ref[t : t + 1, :] == rows, w_ref[t : t + 1, :], 0)
                for f in range(FIELDS):
                    field = (acc >> (6 * f)) & 63
                    ct[pl.ds(f * LO + part * half_lo, half_lo), pl.ds(side * 128, 128)] = (
                        field.astype(F32).astype(BF16)
                    )
        pooled = lax.dot_general(
            ct[...], table[...], (((0,), (0,)), ((), ())), preferred_element_type=F32
        )
        parts[pair] = pooled.reshape(4, 2, HALF, D)
        pair_copy(pair).start()

    def finish_pair(pair):
        pair_copy(pair).wait()
        both = parts[pair, :, c] + s_recv[pair]
        keep[pair] = both
        pack_rows(both, q_out.at[pair])
        for side in range(2):
            i, d = block_of(2 * pair + side)

            @pl.when(d != 0)
            def _():
                ra_copy(i, d, pair, side).start()

            @pl.when(i != 0)
            def _():
                rb_copy(i, d, pick(i, row_steps), pair, side).start()

    def pool_step(pair, carry):
        @pl.when(pair == 2)
        def _():
            info_copy(2).wait()

        @pl.when(pair == 3)
        def _():
            info_copy(3).wait()

        @pl.when(pair == 4)
        def _():
            info_copy(1).wait()

        pool_pair(pair)

        @pl.when(pair > 0)
        def _():
            finish_pair(pair - 1)

        return carry

    lax.fori_loop(0, TILES, pool_step, 0)

    def kept(i, d, half):
        pair, side = place_of[i, d]
        return keep[pair, 2 * side + half]

    second = []
    for d in (2, 1, 3):
        for i in (1, 2, 3):
            rb_copy(i, d, row_steps[i], *place_of[i, d]).wait()
    for d in (2, 1, 3):
        total = kept(0, d, 1)
        for i in (1, 2, 3):
            total = total + unpack_rows(rb.at[i - 1, d])
        pack_rows(total, qb2.at[d - 1])
    for d in (2, 1, 3):
        second.append(send(qb2.at[d - 1], rb2.at[d - 1], r2_s.at[1, d - 1], r2_r.at[1, d - 1], at_x(d)))
    for i in (1, 2, 3):
        for d in (2, 1, 3):
            ra_copy(i, d, *place_of[i, d]).wait()
    from_x = [sum(unpack_rows(ra.at[i, d]) for d in range(3)) for i in (1, 2, 3)]
    finish_pair(TILES - 1)
    for i in (1, 2, 3):
        pack_rows(kept(i, 0, 0) + from_x[i - 1], qa2.at[i - 1])
    for i in (1, 2, 3):
        second.append(
            send(qa2.at[i - 1], ra2.at[i - 1], r2_s.at[0, i - 1], r2_r.at[0, i - 1], at_y(row_steps[i]))
        )

    before = (
        lax.broadcasted_iota(jnp.int32, (128, 128), 0) < lax.broadcasted_iota(jnp.int32, (128, 128), 1)
    ).astype(F32).astype(BF16)
    ones = jnp.ones((128, 128), BF16)
    block_ids = lax.broadcasted_iota(jnp.int32, (BLKS, 128), 0) + label * BLKS
    low_lanes = lax.broadcasted_iota(jnp.int32, (INFO - SEQ, 128), 1) < Q_DEV
    running = jnp.zeros((BLKS, 128), F32)
    for j in range(2 * TILES):
        tile, p = j // 2, j % 2
        if tile < NY:
            left = info[tile, 2 * p, SEQ:INFO, :].astype(jnp.int32)
            right = info[tile, 2 * p + 1, SEQ:INFO, :].astype(jnp.int32)
            lists = jnp.where(low_lanes, left, pltpu.roll(right, Q_DEV, 1))
        else:
            left = info[2 * p, tile - NY, SEQ:INFO, :].astype(jnp.int32)
            right = info[2 * p + 1, tile - NY, SEQ:INFO, :].astype(jnp.int32)
            lists = jnp.where(low_lanes, pltpu.roll(left, Q_DEV, 1), right)
        hit = jnp.zeros((BLKS, 128), F32)
        place = jnp.zeros((BLKS, 128), F32)
        for k in range(K):
            same = lists[k : k + 1, :] == block_ids
            hit = hit + jnp.where(same, 1.0, 0.0)
            if k < POS:
                at_row = lists[K + k : K + k + 1, :].astype(F32) + 1.0
                place = place + jnp.where(same, at_row, 0.0)
        hit16 = hit.astype(BF16)
        ahead = jnp.dot(hit16, before, preferred_element_type=F32) + running
        running = running + jnp.dot(hit16, ones, preferred_element_type=F32)
        rank[:, j, :] = jnp.where(hit > 0.0, ahead, -1.0)
        off2[:, j, :] = hit + place

    slot_ids = lax.broadcasted_iota(jnp.int32, (GCAP, 128), 0).astype(F32)

    def one_hot(b, carry):
        rows = pl.ds(pl.multiple_of(b * GCAP, GCAP), GCAP)
        found = jnp.zeros((GCAP, 128), F32)
        for j in range(2 * TILES):
            lanes = slice((j % 2) * 128, (j % 2 + 1) * 128)
            same = rank[b, j : j + 1, :] == slot_ids
            onehot[j // 2, rows, lanes] = jnp.where(same, 1.0, 0.0).astype(BF16)
            found = found + jnp.where(same, off2[b, j : j + 1, :], 0.0)
        slot_off[rows, :] = jnp.broadcast_to(jnp.sum(found, axis=1, keepdims=True), (GCAP, 128))
        return carry

    lax.fori_loop(0, BLKS // 2, one_hot, 0)

    for d in (1, 3, 2):
        ra_copy(0, d, *place_of[0, d]).wait()
    for copy in second[0:3]:
        copy.wait()
    near = [
        kept(0, 0, 0) + sum(unpack_rows(ra.at[0, n]) for n in range(3)),
        kept(0, 0, 1) + sum(unpack_rows(rb2.at[n]) for n in range(3)),
    ]
    for i in (1, 2, 3):
        rb_copy(i, 0, row_steps[i], *place_of[i, 0]).wait()
    for copy in second[3:6]:
        copy.wait()
    gain = gain_ref[...].reshape(1, D)
    for half in range(2):
        pooled = near[half]
        for n in range(3):
            pooled = pooled + unpack_rows(ra2.at[n] if half == 0 else rb.at[n, 0])
        pooled = pooled / SEQ
        scale = lax.rsqrt(jnp.mean(pooled * pooled, axis=-1, keepdims=True) + 1e-06)
        value = (pooled * scale * gain).astype(BF16)
        if half == 0:
            emb[y, x, c] = value
        else:
            emb[NY + x, y, c] = value

    def ex_copy(half, d):
        mine = emb.at[y, x, c] if half == 0 else emb.at[NY + x, y, c]
        return remote(mine, mine, ex_s.at[half, d - 1], ex_r.at[half, d - 1], at_x(d) if half == 0 else at_y(d))

    def ey_copy(half, back, d):
        if half == 0:
            piece, device = emb.at[y, lax.rem(x + NX - back, NX), c], at_y(d)
        else:
            piece, device = emb.at[NY + x, lax.rem(y + NY - back, NY), c], at_x(d)
        return remote(piece, piece, ey_s.at[half, back, d - 1], ey_r.at[half, back, d - 1], device)

    halves = (0, 1)
    for d in (1, 3, 2):
        for half in halves:
            ex_copy(half, d).start()
    lax.fori_loop(BLKS // 2, BLKS, one_hot, 0)
    for d in (1, 3):
        for half in halves:
            ey_copy(half, 0, d).start()
    for back in (1, 3, 2):
        for half in halves:
            ex_copy(half, back).wait()
            for d in (1, 3):
                ey_copy(half, back, d).start()

    def relay_copy(half, back, side):
        rows = pl.ds(side * (HALF // 2), HALF // 2)
        step = 1 if side == 0 else 3
        if half == 0:
            piece = emb.at[lax.rem(y + NY - step, NY), lax.rem(x + NX - back, NX), c, rows]
            device = at_y(step)
        else:
            piece = emb.at[NY + lax.rem(x + NX - step, NX), lax.rem(y + NY - back, NY), c, rows]
            device = at_x(step)
        return remote(piece, piece, er_s.at[half, back, side], er_r.at[half, back, side], device)

    def relay(back):
        for side in range(2):
            for half in halves:
                ey_copy(half, back, 1 if side == 0 else 3).wait()
                relay_copy(half, back, side).start()

    def forward(d):
        row = emb.at[lax.rem(y + NY - d, NY), :, c]
        col = emb.at[NY + lax.rem(x + NX - d, NX), :, c]
        return [
            send(row, row, es_s.at[0, d], es_r.at[0, d], sibling),
            send(col, col, es_s.at[1, d], es_r.at[1, d], sibling),
        ]

    pair_rows = 2 * GCAP
    chunk = SLOTS // 2

    def partial_slots(d, rows):
        tile_a = lax.rem(y + NY - d, NY)
        tile_b = NY + lax.rem(x + NX - d, NX)
        return jnp.dot(
            onehot[tile_a, rows, :], emb[tile_a].reshape(TILE, D), preferred_element_type=F32
        ) + jnp.dot(onehot[tile_b, rows, :], emb[tile_b].reshape(TILE, D), preferred_element_type=F32)

    def gather_slots(d):
        def body(m, carry):
            rows = pl.ds(pl.multiple_of(m * chunk, chunk), chunk)
            value = partial_slots(d, rows)
            eacc[rows, :] = value if d == 0 else value + eacc[rows, :]
            return carry

        lax.fori_loop(0, SLOTS // chunk, body, 0)

    def all_wait(copies):
        for copy in copies:
            copy.wait()

    moving = forward(0)
    relay(0)
    all_wait(moving)
    gather_slots(0)
    for back in (1, 3, 2):
        relay(back)
    moving = forward(1)
    moving_3 = forward(3)
    all_wait(moving)
    gather_slots(1)
    all_wait(moving_3)
    moving = []
    for back in (0, 1, 3, 2):
        for half in halves:
            for side in range(2):
                relay_copy(half, back, side).wait()
            if half == 0:
                piece = emb.at[lax.rem(y + 2, NY), lax.rem(x + NX - back, NX), c]
            else:
                piece = emb.at[NY + lax.rem(x + 2, NX), lax.rem(y + NY - back, NY), c]
            moving.append(send(piece, piece, ef_s.at[half, back], ef_r.at[half, back], sibling))
    gather_slots(3)
    all_wait(moving)
    load_slab.wait()

    row_ids = lax.broadcasted_iota(jnp.int32, (pair_rows, 2 * BLOCK), 0)
    col_ids = lax.broadcasted_iota(jnp.int32, (pair_rows, 2 * BLOCK), 1)
    same_block = (row_ids >= GCAP) == (col_ids >= BLOCK)
    col_in = jnp.where(col_ids >= BLOCK, col_ids - BLOCK, col_ids).astype(F32) + 2.0

    def grads(offset):
        dest = lax.rem(z + offset + NZ, NZ)
        srows = pl.ds(pl.multiple_of(dest * pair_rows, pair_rows), pair_rows)
        lrows = pl.ds(pl.multiple_of(dest * 2 * BLOCK, 2 * BLOCK), 2 * BLOCK)
        es_rows = eacc[srows, :]
        if offset == 4:
            es_rows = es_rows + partial_slots(2, srows)
        es_rows = es_rows.astype(BF16)
        labels = slab[lrows, :]
        logits = lax.dot_general(es_rows, labels, (((1,), (1,)), ((), ())), preferred_element_type=F32)
        seen = slot_off[srows, :]
        seen = jnp.concatenate([seen, seen], axis=1)
        g = jax.nn.sigmoid(logits) - jnp.where(seen == col_in, 1.0, 0.0)
        g = jnp.where(same_block & (seen > 0.0), g, 0.0).astype(BF16)
        part = lax.dot_general(g, es_rows, (((0,), (0,)), ((), ())), preferred_element_type=F32)
        if offset == 4:
            for way in range(2):
                zsend[way, 0, way] = part[way * BLOCK : (way + 1) * BLOCK, :].astype(BF16)
                z_send(way, 0, way)
        hgrad[srows, :] = jnp.dot(g, labels, preferred_element_type=F32).astype(BF16)
        return part

    zc = {}

    def z_send(way, step, sub):
        zc[way, step, sub] = send(
            zsend.at[way, step, sub], zrecv.at[way, step, sub],
            z_s.at[way, step, sub], z_r.at[way, step, sub], up if way == 0 else down,
        )

    def z_fill(way, step, sub, with_recv):
        value = parts[3 * way + step - 1, pl.ds(2 * sub, 2)].reshape(BLOCK, D)
        if with_recv:
            value = value + zrecv[way, step - 1, sub].astype(F32)
        zsend[way, step, sub] = value.astype(BF16)
        z_send(way, step, sub)

    def z_pass(step, first):
        for way in range(2):
            sub = 1 - way if first else way
            zc[way, step - 1, sub].wait()
            z_fill(way, step, sub, True)

    grads(4)
    gather_slots(2)
    for way, sign in ((0, 1), (1, -1)):
        parts[3 * way] = grads(3 * sign).reshape(4, 2, HALF, D)
        z_fill(way, 1, 1 - way, False)
    for step in (2, 3):
        for way, sign in ((0, 1), (1, -1)):
            parts[3 * way + step - 1] = grads((4 - step) * sign).reshape(4, 2, HALF, D)
    sg_ref[...] = grads(0)
    z_pass(1, False)

    def spread(tiles):
        def body(k, carry):
            grad = lax.dot_general(
                onehot[k], hgrad[...], (((0,), (0,)), ((), ())), preferred_element_type=F32
            )
            tmp[...] = grad.reshape(4, 2, HALF, D)
            for side in range(4):
                g_own[k, side] = tmp[side, c]
                g_send[k, side] = tmp[side, o].astype(BF16)
            send(g_send.at[k], g_recv.at[k], gp_s.at[k], gp_r.at[k], sibling)
            return carry

        lax.fori_loop(tiles[0], tiles[1], body, 0)

    gx = {}

    def to_chips(k):
        pltpu.make_async_remote_copy(
            src_ref=g_send.at[k], dst_ref=g_recv.at[k], send_sem=gp_s.at[k],
            recv_sem=gp_r.at[k], device_id=sibling, device_id_type=MESH,
        ).wait()
        for d in (2, 1, 3, 0):
            if k < NY:
                piece, device = lax.rem(x + d, NX), at_x(d)
            else:
                piece, device = lax.rem(y + d, NY), at_y(d)
            both = g_own[k, piece] + g_recv[k, piece].astype(F32)
            if d == 0:
                g_own[k, 0] = both
            else:
                gx_send[k, d - 1] = both.astype(BF16)
                gx[k, d] = send(
                    gx_send.at[k, d - 1], gx_recv.at[k, d - 1], gx_s.at[k, d - 1], gx_r.at[k, d - 1], device
                )

    spread((0, 2))
    spread((4, 6))
    z_pass(2, True)
    for k in (0, 4, 1, 5):
        to_chips(k)
    spread((2, 4))
    spread((6, 8))
    z_pass(2, False)
    for k in (2, 6, 3, 7):
        to_chips(k)
    z_pass(3, True)

    def own_total(k):
        total = g_own[k, 0]
        for d in (1, 3, 2):
            total = total + gx_recv[k, d - 1].astype(F32)
        return total

    for k in range(TILES):
        for d in (1, 3, 2):
            gx[k, d].wait()
    z_pass(3, False)
    copies = []
    for d in (2, 1, 3):
        pack_rows(own_total(lax.rem(y + d, NY)), gy_send.at[0, d - 1])
        copies.append(send(gy_send.at[0, d - 1], gy_recv.at[0, d - 1], gy_s.at[0, d - 1], gy_r.at[0, d - 1], at_y(d)))
        pack_rows(own_total(NY + lax.rem(x + d, NX)), gy_send.at[1, d - 1])
        copies.append(send(gy_send.at[1, d - 1], gy_recv.at[1, d - 1], gy_s.at[1, d - 1], gy_r.at[1, d - 1], at_x(d)))
    eg_ref[0:HALF, :] = own_total(y)
    eg_ref[HALF:Q_DEV, :] = own_total(NY + x)

    def ring_end(way, sub):
        zc[way, 3, sub].wait()
        rows = pl.ds(sub * BLOCK, BLOCK)
        sg_ref[rows, :] = sg_ref[rows, :] + zrecv[way, 3, sub].astype(F32)

    for way in range(2):
        ring_end(way, 1 - way)
    for copy in copies:
        copy.wait()
    for half in range(2):
        rows = pl.ds(half * HALF, HALF)
        eg_ref[rows, :] = eg_ref[rows, :] + sum(unpack_rows(gy_recv.at[half, n]) for n in range(3))
    for way in range(2):
        ring_end(way, way)


def hand_over(eg_ref, sg_ref, eg_out, sg_out):
    eg_out[...] = eg_ref[...]
    sg_out[...] = sg_ref[...].reshape(2 * BLOCK, 1, D)


def local(token_ids, token_table, norm_gain, slab, shortlist, positive_offsets):
    vmem = pl.BlockSpec(memory_space=pltpu.VMEM)
    anyspace = pl.BlockSpec(memory_space=pl.ANY)
    dma = pltpu.SemaphoreType.DMA
    i16 = jnp.int16
    scratch = dict(
        tok_ref=pltpu.VMEM((SEQ, Q_DEV), jnp.int32),
        list_ref=pltpu.VMEM((K, Q_DEV), jnp.int32),
        pos_ref=pltpu.VMEM((POS, Q_DEV), jnp.int32),
        gain_ref=pltpu.VMEM((D,), F32),
        table=pltpu.VMEM((VOC_PAD, D), BF16),
        slab=pltpu.VMEM((BLKS * BLOCK, D), BF16),
        stage=pltpu.VMEM((INFO, 128), jnp.int32),
        row_info=pltpu.VMEM((NX, 2, INFO, 128), i16),
        info=pltpu.VMEM((NY, NX, INFO, 128), i16),
        lo_ref=pltpu.VMEM((SEQ, 128), jnp.int32),
        w_ref=pltpu.VMEM((SEQ, 128), jnp.int32),
        ct=pltpu.VMEM((VOC_PAD, 256), BF16),
        tmp=pltpu.VMEM((4, 2, HALF, D), F32),
        parts=pltpu.VMEM((TILES, 4, 2, HALF, D), F32),
        s_recv=pltpu.VMEM((TILES, 4, HALF, D), F32),
        keep=pltpu.VMEM((TILES, 4, HALF, D), F32),
        q_out=pltpu.VMEM((TILES, 4, HALF, Q_COLS), i16),
        ra=pltpu.VMEM((NY, 3, HALF, Q_COLS), i16),
        rb=pltpu.VMEM((3, NX, HALF, Q_COLS), i16),
        qa2=pltpu.VMEM((3, HALF, Q_COLS), i16),
        ra2=pltpu.VMEM((3, HALF, Q_COLS), i16),
        qb2=pltpu.VMEM((3, HALF, Q_COLS), i16),
        rb2=pltpu.VMEM((3, HALF, Q_COLS), i16),
        emb=pltpu.VMEM((TILES, 4, 2, HALF, D), BF16),
        rank=pltpu.VMEM((BLKS, 2 * TILES, 128), F32),
        off2=pltpu.VMEM((BLKS, 2 * TILES, 128), F32),
        onehot=pltpu.VMEM((TILES, SLOTS, TILE), BF16),
        slot_off=pltpu.VMEM((SLOTS, 128), F32),
        eacc=pltpu.VMEM((SLOTS, D), F32),
        hgrad=pltpu.VMEM((SLOTS, D), BF16),
        zsend=pltpu.VMEM((2, 4, 2, BLOCK, D), BF16),
        zrecv=pltpu.VMEM((2, 4, 2, BLOCK, D), BF16),
        g_own=pltpu.VMEM((TILES, 4, HALF, D), F32),
        g_send=pltpu.VMEM((TILES, 4, HALF, D), BF16),
        g_recv=pltpu.VMEM((TILES, 4, HALF, D), BF16),
        gx_send=pltpu.VMEM((TILES, 3, HALF, D), BF16),
        gx_recv=pltpu.VMEM((TILES, 3, HALF, D), BF16),
        gy_send=pltpu.VMEM((2, 3, HALF, Q_COLS), i16),
        gy_recv=pltpu.VMEM((2, 3, HALF, Q_COLS), i16),
        load_sem=dma((6,)),
        info_s=dma((11,)), info_r=dma((11,)),
        pair_s=dma((TILES,)), pair_r=dma((TILES,)),
        ra_s=dma((NY, 3)), ra_r=dma((NY, 3)), rb_s=dma((3, NX)), rb_r=dma((3, NX)),
        r2_s=dma((2, 3)), r2_r=dma((2, 3)),
        ex_s=dma((2, 3)), ex_r=dma((2, 3)), ey_s=dma((2, 4, 3)), ey_r=dma((2, 4, 3)),
        es_s=dma((2, 4)), es_r=dma((2, 4)), er_s=dma((2, 4, 2)), er_r=dma((2, 4, 2)), ef_s=dma((2, 4)), ef_r=dma((2, 4)),
        z_s=dma((2, 4, 2)), z_r=dma((2, 4, 2)),
        gp_s=dma((TILES,)), gp_r=dma((TILES,)),
        gx_s=dma((TILES, 3)), gx_r=dma((TILES, 3)), gy_s=dma((2, 3)), gy_r=dma((2, 3)),
    )
    eg, sg = pl.pallas_call(
        kernel,
        out_shape=(
            jax.ShapeDtypeStruct((Q_DEV, D), F32),
            jax.ShapeDtypeStruct((2 * BLOCK, D), F32),
        ),
        in_specs=[anyspace] * 6,
        out_specs=(vmem, vmem),
        scratch_shapes=list(scratch.values()),
        compiler_params=pltpu.CompilerParams(
            collective_id=0, has_side_effects=True, vmem_limit_bytes=57 << 20
        ),
    )(token_ids.T, shortlist.T, positive_offsets.T, norm_gain, token_table, slab)
    return pl.pallas_call(
        hand_over,
        out_shape=(
            jax.ShapeDtypeStruct((Q_DEV, D), F32),
            jax.ShapeDtypeStruct((2 * BLOCK, 1, D), F32),
        ),
        in_specs=[vmem, vmem],
        out_specs=(vmem, vmem),
    )(eg, sg)


def solution(mesh):
    return jax.shard_map(
        local,
        mesh=mesh,
        in_specs=(
            P(("dp", "label"), None),
            P("label", None),
            P(),
            P("label", None),
            P(("dp", "label"), None),
            P(("dp", "label"), None),
        ),
        out_specs=(P(("dp", "label"), None), P("dp", "label", None)),
        check_vma=False,
    )
```

```python
import math

import jax
import jax.numpy as jnp
from jax import lax
from jax.experimental import pallas as pl
from jax.experimental.pallas import tpu as pltpu
from jax.sharding import PartitionSpec as P

K = 8
POS = 2
BLOCK = 128
GCAP = 96
SEQ = 32
NX = 4
NY = 4
NZ = 8
CHIPS = NX * NY
Q_DEV = 64
Q_CHIP = 2 * Q_DEV
GROUP = CHIPS * Q_CHIP
VOC = 952
VOC_PAD = 960
LO = 192
FIELDS = 5
D = 768
BLKS = 16
SLOTS = BLKS * GCAP
HALF = Q_DEV // 2
INFO = 48
TILES = 8
TILE = 256
Q_COLS = D + 128
TOP = 32000.0
MESH = pl.DeviceIdType.MESH
F32 = jnp.float32
BF16 = jnp.bfloat16


def pack_rows(value, dst):
    largest = jnp.max(jnp.abs(value), axis=-1, keepdims=True)
    step = jnp.ceil(jnp.log(jnp.maximum(largest, 1e-30)) * (8.0 / math.log(2.0)))
    factor = jnp.exp(step * (-math.log(2.0) / 8.0)) * TOP
    dst[..., 0:D] = jnp.round(value * factor).astype(jnp.int32).astype(jnp.int16)
    dst[..., D:Q_COLS] = jnp.broadcast_to(step, value.shape[:-1] + (128,)).astype(jnp.int32).astype(jnp.int16)


def unpack_rows(src):
    step = src[..., D : D + 1].astype(jnp.int32).astype(F32)
    factor = jnp.exp(step * (math.log(2.0) / 8.0)) * (1.0 / TOP)
    return src[..., 0:D].astype(jnp.int32).astype(F32) * factor


def kernel(
    tok_hbm, list_hbm, pos_hbm, gain_hbm, table_hbm, slab_hbm,
    eg_ref, sg_ref,
    tok_ref, list_ref, pos_ref, gain_ref, table, slab, stage, row_info, info, lo_ref, w_ref, ct, tmp,
    parts, s_recv, keep, q_out, ra, rb, qa2, ra2, qb2, rb2,
    emb, rank, off2, onehot, slot_off, eacc, hgrad,
    zsend, zrecv,
    g_own, g_send, g_recv, gx_send, gx_recv, gy_send, gy_recv,
    load_sem, info_s, info_r, pair_s, pair_r, ra_s, ra_r, rb_s, rb_r, r2_s, r2_r,
    ex_s, ex_r, ey_s, ey_r, es_s, es_r, er_s, er_r, ef_s, ef_r, z_s, z_r,
    gp_s, gp_r, gx_s, gx_r, gy_s, gy_r,
):
    z = lax.axis_index("dp")
    label = lax.axis_index("label")
    y = lax.div(label, 2 * NX)
    x = lax.rem(lax.div(label, 2), NX)
    c = lax.rem(label, 2)
    o = 1 - c

    def lab(yy, xx, cc):
        return (yy * NX + xx) * 2 + cc

    def at_x(dx):
        return (z, lab(y, lax.rem(x + dx, NX), c))

    def at_y(dy):
        return (z, lab(lax.rem(y + dy, NY), x, c))

    sibling = (z, lab(y, x, o))
    up = (lax.rem(z + 1, NZ), label)
    down = (lax.rem(z + NZ - 1, NZ), label)

    def remote(src, dst, ssem, rsem, device):
        return pltpu.make_async_remote_copy(
            src_ref=src, dst_ref=dst, send_sem=ssem, recv_sem=rsem,
            device_id=device, device_id_type=MESH,
        )

    def send(src, dst, ssem, rsem, device):
        copy = remote(src, dst, ssem, rsem, device)
        copy.start()
        return copy

    barrier = pltpu.get_barrier_semaphore()
    row_peers = [(z, lab(y, lax.rem(x + d, NX), cc)) for d in (2, 1, 3) for cc in (c, o)]
    peers = row_peers + [sibling, up, down] + [at_y(d) for d in (1, 2, 3)]
    for device in peers:
        pl.semaphore_signal(barrier, inc=1, device_id=device, device_id_type=MESH)

    loads = [
        pltpu.make_async_copy(tok_hbm, tok_ref, load_sem.at[2]),
        pltpu.make_async_copy(list_hbm, list_ref, load_sem.at[3]),
        pltpu.make_async_copy(pos_hbm, pos_ref, load_sem.at[4]),
        pltpu.make_async_copy(gain_hbm, gain_ref, load_sem.at[5]),
    ]
    load_table = pltpu.make_async_copy(table_hbm, table.at[pl.ds(0, VOC)], load_sem.at[0])
    load_slab = pltpu.make_async_copy(slab_hbm, slab, load_sem.at[1])
    for load in loads + [load_table, load_slab]:
        load.start()

    stage[...] = jnp.zeros_like(stage)
    for load in loads:
        load.wait()
    for core in range(2):

        @pl.when(c == core)
        def _():
            for half in range(2):
                src = slice(half * HALF, (half + 1) * HALF)
                dst = slice(half * Q_DEV + core * HALF, half * Q_DEV + (core + 1) * HALF)
                stage[0:SEQ, dst] = tok_ref[:, src]
                stage[SEQ : SEQ + K, dst] = list_ref[:, src]
                stage[SEQ + K : SEQ + K + POS, dst] = pos_ref[:, src]

    row_info[0, 0] = stage[...].astype(jnp.int16)
    pl.semaphore_wait(barrier, len(peers))

    copies = []
    for d in (2, 1, 3):
        for s in range(2):
            copies.append(
                send(
                    row_info.at[0, 0], row_info.at[d, s], info_s.at[2 * d + s], info_r.at[2 * d + s],
                    (z, lab(y, lax.rem(x + d, NX), o if s else c)),
                )
            )
    copies.append(send(row_info.at[0, 0], row_info.at[0, 1], info_s.at[1], info_r.at[1], sibling))
    load_table.wait()
    table[VOC:VOC_PAD, :] = jnp.zeros((VOC_PAD - VOC, D), BF16)
    for copy in copies:
        copy.wait()
    for d in range(NX):
        both = row_info[d, 0].astype(jnp.int32) + row_info[d, 1].astype(jnp.int32)
        info[y, lax.rem(x + NX - d, NX)] = both.astype(jnp.int16)

    def info_copy(d):
        return remote(info.at[y], info.at[y], info_s.at[7 + d], info_r.at[7 + d], at_y(d))

    for d in (2, 1, 3):
        info_copy(d).start()

    base = label * VOC
    half_lo = LO // 2
    row_steps = (0, 2, 1, 3)

    def pick(index, values):
        value = values[-1]
        for n in range(len(values) - 2, -1, -1):
            value = jnp.where(index == n, values[n], value)
        return value

    order = [(0, d) for d in (2, 1, 3, 0)] + [(i, d) for i in (1, 2, 3) for d in (2, 1, 3)]
    order += [(i, 0) for i in (1, 2, 3)]
    place_of = {block: divmod(n, 2) for n, block in enumerate(order)}

    def block_of(n):
        rest = jnp.maximum(n - 4, 0)
        i = jnp.where(n < 4, 0, jnp.where(n < 13, 1 + lax.div(rest, 3), n - 12))
        third = jnp.where(n < 4, n, lax.rem(rest, 3))
        d = jnp.where(n >= 13, 0, pick(third, (2, 1, 3, 0)))
        return i, d

    def pair_copy(pair):
        return remote(parts.at[pair, :, o], s_recv.at[pair], pair_s.at[pair], pair_r.at[pair], sibling)

    def ra_copy(i, d, pair, side):
        return remote(q_out.at[pair, 2 * side], ra.at[i, d - 1], ra_s.at[i, d - 1], ra_r.at[i, d - 1], at_x(d))

    def rb_copy(i, d, step, pair, side):
        return remote(
            q_out.at[pair, 2 * side + 1], rb.at[i - 1, d], rb_s.at[i - 1, d], rb_r.at[i - 1, d], at_y(step)
        )

    def pool_pair(pair):
        for side in range(2):
            i, d = block_of(2 * pair + side)
            chip_y, chip_x = lax.rem(y + pick(i, row_steps), NY), lax.rem(x + d, NX)
            ids = info[chip_y, chip_x, 0:SEQ, :].astype(jnp.int32) - base
            valid = (ids >= 0) & (ids < VOC)
            high = (ids * 683) >> 17
            weight = jnp.ones_like(ids)
            for f in range(1, FIELDS):
                weight = jnp.where(high == f, 1 << (6 * f), weight)
            lo_ref[...] = jnp.where(valid, ids - high * LO, -1)
            w_ref[...] = jnp.where(valid, weight, 0)
            for part in range(2):
                rows = lax.broadcasted_iota(jnp.int32, (half_lo, 128), 0) + part * half_lo
                acc = jnp.zeros((half_lo, 128), jnp.int32)
                for t in range(SEQ):
                    acc = acc + jnp.where(lo_ref[t : t + 1, :] == rows, w_ref[t : t + 1, :], 0)
                for f in range(FIELDS):
                    field = (acc >> (6 * f)) & 63
                    ct[pl.ds(f * LO + part * half_lo, half_lo), pl.ds(side * 128, 128)] = (
                        field.astype(F32).astype(BF16)
                    )
        pooled = lax.dot_general(
            ct[...], table[...], (((0,), (0,)), ((), ())), preferred_element_type=F32
        )
        parts[pair] = pooled.reshape(4, 2, HALF, D)
        pair_copy(pair).start()

    def finish_pair(pair):
        pair_copy(pair).wait()
        both = parts[pair, :, c] + s_recv[pair]
        keep[pair] = both
        pack_rows(both, q_out.at[pair])
        for side in range(2):
            i, d = block_of(2 * pair + side)

            @pl.when(d != 0)
            def _():
                ra_copy(i, d, pair, side).start()

            @pl.when(i != 0)
            def _():
                rb_copy(i, d, pick(i, row_steps), pair, side).start()

    def pool_step(pair, carry):
        @pl.when(pair == 2)
        def _():
            info_copy(2).wait()

        @pl.when(pair == 3)
        def _():
            info_copy(3).wait()

        @pl.when(pair == 4)
        def _():
            info_copy(1).wait()

        pool_pair(pair)

        @pl.when(pair > 0)
        def _():
            finish_pair(pair - 1)

        return carry

    lax.fori_loop(0, TILES, pool_step, 0)

    def kept(i, d, half):
        pair, side = place_of[i, d]
        return keep[pair, 2 * side + half]

    second = []
    for d in (2, 1, 3):
        for i in (1, 2, 3):
            rb_copy(i, d, row_steps[i], *place_of[i, d]).wait()
    for d in (2, 1, 3):
        total = kept(0, d, 1)
        for i in (1, 2, 3):
            total = total + unpack_rows(rb.at[i - 1, d])
        pack_rows(total, qb2.at[d - 1])
    for d in (2, 1, 3):
        second.append(send(qb2.at[d - 1], rb2.at[d - 1], r2_s.at[1, d - 1], r2_r.at[1, d - 1], at_x(d)))
    for i in (1, 2, 3):
        for d in (2, 1, 3):
            ra_copy(i, d, *place_of[i, d]).wait()
    from_x = [sum(unpack_rows(ra.at[i, d]) for d in range(3)) for i in (1, 2, 3)]
    finish_pair(TILES - 1)
    for i in (1, 2, 3):
        pack_rows(kept(i, 0, 0) + from_x[i - 1], qa2.at[i - 1])
    for i in (1, 2, 3):
        second.append(
            send(qa2.at[i - 1], ra2.at[i - 1], r2_s.at[0, i - 1], r2_r.at[0, i - 1], at_y(row_steps[i]))
        )

    before = (
        lax.broadcasted_iota(jnp.int32, (128, 128), 0) < lax.broadcasted_iota(jnp.int32, (128, 128), 1)
    ).astype(F32).astype(BF16)
    ones = jnp.ones((128, 128), BF16)
    block_ids = lax.broadcasted_iota(jnp.int32, (BLKS, 128), 0) + label * BLKS
    low_lanes = lax.broadcasted_iota(jnp.int32, (INFO - SEQ, 128), 1) < Q_DEV
    running = jnp.zeros((BLKS, 128), F32)
    for j in range(2 * TILES):
        tile, p = j // 2, j % 2
        if tile < NY:
            left = info[tile, 2 * p, SEQ:INFO, :].astype(jnp.int32)
            right = info[tile, 2 * p + 1, SEQ:INFO, :].astype(jnp.int32)
            lists = jnp.where(low_lanes, left, pltpu.roll(right, Q_DEV, 1))
        else:
            left = info[2 * p, tile - NY, SEQ:INFO, :].astype(jnp.int32)
            right = info[2 * p + 1, tile - NY, SEQ:INFO, :].astype(jnp.int32)
            lists = jnp.where(low_lanes, pltpu.roll(left, Q_DEV, 1), right)
        hit = jnp.zeros((BLKS, 128), F32)
        place = jnp.zeros((BLKS, 128), F32)
        for k in range(K):
            same = lists[k : k + 1, :] == block_ids
            hit = hit + jnp.where(same, 1.0, 0.0)
            if k < POS:
                at_row = lists[K + k : K + k + 1, :].astype(F32) + 1.0
                place = place + jnp.where(same, at_row, 0.0)
        hit16 = hit.astype(BF16)
        ahead = jnp.dot(hit16, before, preferred_element_type=F32) + running
        running = running + jnp.dot(hit16, ones, preferred_element_type=F32)
        rank[:, j, :] = jnp.where(hit > 0.0, ahead, -1.0)
        off2[:, j, :] = hit + place

    slot_ids = lax.broadcasted_iota(jnp.int32, (GCAP, 128), 0).astype(F32)

    def one_hot(b, carry):
        rows = pl.ds(pl.multiple_of(b * GCAP, GCAP), GCAP)
        found = jnp.zeros((GCAP, 128), F32)
        for j in range(2 * TILES):
            lanes = slice((j % 2) * 128, (j % 2 + 1) * 128)
            same = rank[b, j : j + 1, :] == slot_ids
            onehot[j // 2, rows, lanes] = jnp.where(same, 1.0, 0.0).astype(BF16)
            found = found + jnp.where(same, off2[b, j : j + 1, :], 0.0)
        slot_off[rows, :] = jnp.broadcast_to(jnp.sum(found, axis=1, keepdims=True), (GCAP, 128))
        return carry

    lax.fori_loop(0, BLKS // 2, one_hot, 0)

    for d in (1, 3, 2):
        ra_copy(0, d, *place_of[0, d]).wait()
    for copy in second[0:3]:
        copy.wait()
    near = [
        kept(0, 0, 0) + sum(unpack_rows(ra.at[0, n]) for n in range(3)),
        kept(0, 0, 1) + sum(unpack_rows(rb2.at[n]) for n in range(3)),
    ]
    for i in (1, 2, 3):
        rb_copy(i, 0, row_steps[i], *place_of[i, 0]).wait()
    for copy in second[3:6]:
        copy.wait()
    def ex_copy(half, d):
        mine = emb.at[y, x, c] if half == 0 else emb.at[NY + x, y, c]
        return remote(mine, mine, ex_s.at[half, d - 1], ex_r.at[half, d - 1], at_x(d) if half == 0 else at_y(d))

    gain = gain_ref[...].reshape(1, D)
    for half in range(2):
        pooled = near[half]
        for n in range(3):
            pooled = pooled + unpack_rows(ra2.at[n] if half == 0 else rb.at[n, 0])
        pooled = pooled / SEQ
        scale = lax.rsqrt(jnp.mean(pooled * pooled, axis=-1, keepdims=True) + 1e-06)
        value = (pooled * scale * gain).astype(BF16)
        if half == 0:
            emb[y, x, c] = value
        else:
            emb[NY + x, y, c] = value
        for d in (1, 3, 2):
            ex_copy(half, d).start()

    def ey_copy(half, back, d):
        if half == 0:
            piece, device = emb.at[y, lax.rem(x + NX - back, NX), c], at_y(d)
        else:
            piece, device = emb.at[NY + x, lax.rem(y + NY - back, NY), c], at_x(d)
        return remote(piece, piece, ey_s.at[half, back, d - 1], ey_r.at[half, back, d - 1], device)

    halves = (0, 1)
    lax.fori_loop(BLKS // 2, BLKS, one_hot, 0)
    for d in (1, 3):
        for half in halves:
            ey_copy(half, 0, d).start()
    for back in (1, 3, 2):
        for half in halves:
            ex_copy(half, back).wait()
            for d in (1, 3):
                ey_copy(half, back, d).start()

    def relay_copy(half, back, side):
        rows = pl.ds(side * (HALF // 2), HALF // 2)
        step = 1 if side == 0 else 3
        if half == 0:
            piece = emb.at[lax.rem(y + NY - step, NY), lax.rem(x + NX - back, NX), c, rows]
            device = at_y(step)
        else:
            piece = emb.at[NY + lax.rem(x + NX - step, NX), lax.rem(y + NY - back, NY), c, rows]
            device = at_x(step)
        return remote(piece, piece, er_s.at[half, back, side], er_r.at[half, back, side], device)

    def relay(back):
        for side in range(2):
            for half in halves:
                ey_copy(half, back, 1 if side == 0 else 3).wait()
                relay_copy(half, back, side).start()

    def forward(d):
        row = emb.at[lax.rem(y + NY - d, NY), :, c]
        col = emb.at[NY + lax.rem(x + NX - d, NX), :, c]
        return [
            send(row, row, es_s.at[0, d], es_r.at[0, d], sibling),
            send(col, col, es_s.at[1, d], es_r.at[1, d], sibling),
        ]

    pair_rows = 2 * GCAP
    chunk = SLOTS // 2

    def partial_slots(d, rows):
        tile_a = lax.rem(y + NY - d, NY)
        tile_b = NY + lax.rem(x + NX - d, NX)
        return jnp.dot(
            onehot[tile_a, rows, :], emb[tile_a].reshape(TILE, D), preferred_element_type=F32
        ) + jnp.dot(onehot[tile_b, rows, :], emb[tile_b].reshape(TILE, D), preferred_element_type=F32)

    def gather_slots(d):
        def body(m, carry):
            rows = pl.ds(pl.multiple_of(m * chunk, chunk), chunk)
            value = partial_slots(d, rows)
            eacc[rows, :] = value if d == 0 else value + eacc[rows, :]
            return carry

        lax.fori_loop(0, SLOTS // chunk, body, 0)

    def all_wait(copies):
        for copy in copies:
            copy.wait()

    moving = forward(0)
    relay(0)
    all_wait(moving)
    gather_slots(0)
    for back in (1, 3, 2):
        relay(back)
    moving = forward(1)
    moving_3 = forward(3)
    all_wait(moving)
    gather_slots(1)
    all_wait(moving_3)
    moving = []
    for back in (0, 1, 3, 2):
        for half in halves:
            for side in range(2):
                relay_copy(half, back, side).wait()
            if half == 0:
                piece = emb.at[lax.rem(y + 2, NY), lax.rem(x + NX - back, NX), c]
            else:
                piece = emb.at[NY + lax.rem(x + 2, NX), lax.rem(y + NY - back, NY), c]
            moving.append(send(piece, piece, ef_s.at[half, back], ef_r.at[half, back], sibling))
    gather_slots(3)
    all_wait(moving)
    load_slab.wait()

    row_ids = lax.broadcasted_iota(jnp.int32, (pair_rows, 2 * BLOCK), 0)
    col_ids = lax.broadcasted_iota(jnp.int32, (pair_rows, 2 * BLOCK), 1)
    same_block = (row_ids >= GCAP) == (col_ids >= BLOCK)
    col_in = jnp.where(col_ids >= BLOCK, col_ids - BLOCK, col_ids).astype(F32) + 2.0

    def grads(offset):
        dest = lax.rem(z + offset + NZ, NZ)
        srows = pl.ds(pl.multiple_of(dest * pair_rows, pair_rows), pair_rows)
        lrows = pl.ds(pl.multiple_of(dest * 2 * BLOCK, 2 * BLOCK), 2 * BLOCK)
        es_rows = eacc[srows, :]
        if offset == 4:
            es_rows = es_rows + partial_slots(2, srows)
        es_rows = es_rows.astype(BF16)
        labels = slab[lrows, :]
        logits = lax.dot_general(es_rows, labels, (((1,), (1,)), ((), ())), preferred_element_type=F32)
        seen = slot_off[srows, :]
        seen = jnp.concatenate([seen, seen], axis=1)
        g = jax.nn.sigmoid(logits) - jnp.where(seen == col_in, 1.0, 0.0)
        g = jnp.where(same_block & (seen > 0.0), g, 0.0).astype(BF16)
        part = lax.dot_general(g, es_rows, (((0,), (0,)), ((), ())), preferred_element_type=F32)
        if offset == 4:
            for way in range(2):
                zsend[way, 0, way] = part[way * BLOCK : (way + 1) * BLOCK, :].astype(BF16)
                z_send(way, 0, way)
        hgrad[srows, :] = jnp.dot(g, labels, preferred_element_type=F32).astype(BF16)
        return part

    zc = {}

    def z_send(way, step, sub):
        zc[way, step, sub] = send(
            zsend.at[way, step, sub], zrecv.at[way, step, sub],
            z_s.at[way, step, sub], z_r.at[way, step, sub], up if way == 0 else down,
        )

    def z_fill(way, step, sub, with_recv):
        value = parts[3 * way + step - 1, pl.ds(2 * sub, 2)].reshape(BLOCK, D)
        if with_recv:
            value = value + zrecv[way, step - 1, sub].astype(F32)
        zsend[way, step, sub] = value.astype(BF16)
        z_send(way, step, sub)

    def z_pass(step, first):
        for way in range(2):
            sub = 1 - way if first else way
            zc[way, step - 1, sub].wait()
            z_fill(way, step, sub, True)

    grads(4)
    gather_slots(2)
    for way, sign in ((0, 1), (1, -1)):
        parts[3 * way] = grads(3 * sign).reshape(4, 2, HALF, D)
        z_fill(way, 1, 1 - way, False)
    for step in (2, 3):
        for way, sign in ((0, 1), (1, -1)):
            parts[3 * way + step - 1] = grads((4 - step) * sign).reshape(4, 2, HALF, D)
    sg_ref[...] = grads(0)
    z_pass(1, False)

    def spread(tiles):
        def body(k, carry):
            grad = lax.dot_general(
                onehot[k], hgrad[...], (((0,), (0,)), ((), ())), preferred_element_type=F32
            )
            tmp[...] = grad.reshape(4, 2, HALF, D)
            for side in range(4):
                g_own[k, side] = tmp[side, c]
                g_send[k, side] = tmp[side, o].astype(BF16)
            send(g_send.at[k], g_recv.at[k], gp_s.at[k], gp_r.at[k], sibling)
            return carry

        lax.fori_loop(tiles[0], tiles[1], body, 0)

    gx = {}

    def to_chips(k):
        pltpu.make_async_remote_copy(
            src_ref=g_send.at[k], dst_ref=g_recv.at[k], send_sem=gp_s.at[k],
            recv_sem=gp_r.at[k], device_id=sibling, device_id_type=MESH,
        ).wait()
        for d in (2, 1, 3, 0):
            if k < NY:
                piece, device = lax.rem(x + d, NX), at_x(d)
            else:
                piece, device = lax.rem(y + d, NY), at_y(d)
            both = g_own[k, piece] + g_recv[k, piece].astype(F32)
            if d == 0:
                g_own[k, 0] = both
            else:
                gx_send[k, d - 1] = both.astype(BF16)
                gx[k, d] = send(
                    gx_send.at[k, d - 1], gx_recv.at[k, d - 1], gx_s.at[k, d - 1], gx_r.at[k, d - 1], device
                )

    spread((0, 2))
    spread((4, 6))
    z_pass(2, True)
    for k in (0, 4, 1, 5):
        to_chips(k)
    spread((2, 4))
    spread((6, 8))
    z_pass(2, False)
    for k in (2, 6, 3, 7):
        to_chips(k)
    z_pass(3, True)

    def own_total(k):
        total = g_own[k, 0]
        for d in (1, 3, 2):
            total = total + gx_recv[k, d - 1].astype(F32)
        return total

    for k in range(TILES):
        for d in (1, 3, 2):
            gx[k, d].wait()
    z_pass(3, False)
    copies = []
    for d in (2, 1, 3):
        pack_rows(own_total(lax.rem(y + d, NY)), gy_send.at[0, d - 1])
        copies.append(send(gy_send.at[0, d - 1], gy_recv.at[0, d - 1], gy_s.at[0, d - 1], gy_r.at[0, d - 1], at_y(d)))
        pack_rows(own_total(NY + lax.rem(x + d, NX)), gy_send.at[1, d - 1])
        copies.append(send(gy_send.at[1, d - 1], gy_recv.at[1, d - 1], gy_s.at[1, d - 1], gy_r.at[1, d - 1], at_x(d)))
    eg_ref[0:HALF, :] = own_total(y)
    eg_ref[HALF:Q_DEV, :] = own_total(NY + x)

    def ring_end(way, sub):
        zc[way, 3, sub].wait()
        rows = pl.ds(sub * BLOCK, BLOCK)
        sg_ref[rows, :] = sg_ref[rows, :] + zrecv[way, 3, sub].astype(F32)

    for way in range(2):
        ring_end(way, 1 - way)
    for copy in copies:
        copy.wait()
    for half in range(2):
        rows = pl.ds(half * HALF, HALF)
        eg_ref[rows, :] = eg_ref[rows, :] + sum(unpack_rows(gy_recv.at[half, n]) for n in range(3))
    for way in range(2):
        ring_end(way, way)


def hand_over(eg_ref, sg_ref, eg_out, sg_out):
    eg_out[...] = eg_ref[...]
    sg_out[...] = sg_ref[...].reshape(2 * BLOCK, 1, D)


def local(token_ids, token_table, norm_gain, slab, shortlist, positive_offsets):
    vmem = pl.BlockSpec(memory_space=pltpu.VMEM)
    anyspace = pl.BlockSpec(memory_space=pl.ANY)
    dma = pltpu.SemaphoreType.DMA
    i16 = jnp.int16
    scratch = dict(
        tok_ref=pltpu.VMEM((SEQ, Q_DEV), jnp.int32),
        list_ref=pltpu.VMEM((K, Q_DEV), jnp.int32),
        pos_ref=pltpu.VMEM((POS, Q_DEV), jnp.int32),
        gain_ref=pltpu.VMEM((D,), F32),
        table=pltpu.VMEM((VOC_PAD, D), BF16),
        slab=pltpu.VMEM((BLKS * BLOCK, D), BF16),
        stage=pltpu.VMEM((INFO, 128), jnp.int32),
        row_info=pltpu.VMEM((NX, 2, INFO, 128), i16),
        info=pltpu.VMEM((NY, NX, INFO, 128), i16),
        lo_ref=pltpu.VMEM((SEQ, 128), jnp.int32),
        w_ref=pltpu.VMEM((SEQ, 128), jnp.int32),
        ct=pltpu.VMEM((VOC_PAD, 256), BF16),
        tmp=pltpu.VMEM((4, 2, HALF, D), F32),
        parts=pltpu.VMEM((TILES, 4, 2, HALF, D), F32),
        s_recv=pltpu.VMEM((TILES, 4, HALF, D), F32),
        keep=pltpu.VMEM((TILES, 4, HALF, D), F32),
        q_out=pltpu.VMEM((TILES, 4, HALF, Q_COLS), i16),
        ra=pltpu.VMEM((NY, 3, HALF, Q_COLS), i16),
        rb=pltpu.VMEM((3, NX, HALF, Q_COLS), i16),
        qa2=pltpu.VMEM((3, HALF, Q_COLS), i16),
        ra2=pltpu.VMEM((3, HALF, Q_COLS), i16),
        qb2=pltpu.VMEM((3, HALF, Q_COLS), i16),
        rb2=pltpu.VMEM((3, HALF, Q_COLS), i16),
        emb=pltpu.VMEM((TILES, 4, 2, HALF, D), BF16),
        rank=pltpu.VMEM((BLKS, 2 * TILES, 128), F32),
        off2=pltpu.VMEM((BLKS, 2 * TILES, 128), F32),
        onehot=pltpu.VMEM((TILES, SLOTS, TILE), BF16),
        slot_off=pltpu.VMEM((SLOTS, 128), F32),
        eacc=pltpu.VMEM((SLOTS, D), F32),
        hgrad=pltpu.VMEM((SLOTS, D), BF16),
        zsend=pltpu.VMEM((2, 4, 2, BLOCK, D), BF16),
        zrecv=pltpu.VMEM((2, 4, 2, BLOCK, D), BF16),
        g_own=pltpu.VMEM((TILES, 4, HALF, D), F32),
        g_send=pltpu.VMEM((TILES, 4, HALF, D), BF16),
        g_recv=pltpu.VMEM((TILES, 4, HALF, D), BF16),
        gx_send=pltpu.VMEM((TILES, 3, HALF, D), BF16),
        gx_recv=pltpu.VMEM((TILES, 3, HALF, D), BF16),
        gy_send=pltpu.VMEM((2, 3, HALF, Q_COLS), i16),
        gy_recv=pltpu.VMEM((2, 3, HALF, Q_COLS), i16),
        load_sem=dma((6,)),
        info_s=dma((11,)), info_r=dma((11,)),
        pair_s=dma((TILES,)), pair_r=dma((TILES,)),
        ra_s=dma((NY, 3)), ra_r=dma((NY, 3)), rb_s=dma((3, NX)), rb_r=dma((3, NX)),
        r2_s=dma((2, 3)), r2_r=dma((2, 3)),
        ex_s=dma((2, 3)), ex_r=dma((2, 3)), ey_s=dma((2, 4, 3)), ey_r=dma((2, 4, 3)),
        es_s=dma((2, 4)), es_r=dma((2, 4)), er_s=dma((2, 4, 2)), er_r=dma((2, 4, 2)), ef_s=dma((2, 4)), ef_r=dma((2, 4)),
        z_s=dma((2, 4, 2)), z_r=dma((2, 4, 2)),
        gp_s=dma((TILES,)), gp_r=dma((TILES,)),
        gx_s=dma((TILES, 3)), gx_r=dma((TILES, 3)), gy_s=dma((2, 3)), gy_r=dma((2, 3)),
    )
    eg, sg = pl.pallas_call(
        kernel,
        out_shape=(
            jax.ShapeDtypeStruct((Q_DEV, D), F32),
            jax.ShapeDtypeStruct((2 * BLOCK, D), F32),
        ),
        in_specs=[anyspace] * 6,
        out_specs=(vmem, vmem),
        scratch_shapes=list(scratch.values()),
        compiler_params=pltpu.CompilerParams(
            collective_id=0, has_side_effects=True, vmem_limit_bytes=57 << 20
        ),
    )(token_ids.T, shortlist.T, positive_offsets.T, norm_gain, token_table, slab)
    return pl.pallas_call(
        hand_over,
        out_shape=(
            jax.ShapeDtypeStruct((Q_DEV, D), F32),
            jax.ShapeDtypeStruct((2 * BLOCK, 1, D), F32),
        ),
        in_specs=[vmem, vmem],
        out_specs=(vmem, vmem),
    )(eg, sg)


def solution(mesh):
    return jax.shard_map(
        local,
        mesh=mesh,
        in_specs=(
            P(("dp", "label"), None),
            P("label", None),
            P(),
            P("label", None),
            P(("dp", "label"), None),
            P(("dp", "label"), None),
        ),
        out_specs=(P(("dp", "label"), None), P("dp", "label", None)),
        check_vma=False,
    )
```
